256 devices in a mesh: sens: 32 (over x_lo, z, core), hour: 8 (over x_hi, y).
Axes of the slice: x: 4 (x_hi: 2, x_lo: 2; x = x_hi * 2 + x_lo), y: 4, z: 8, core: 2. Of those that a mesh axis runs over, the one named last changes fastest.
Arguments:
- windows: bfloat16 [8, 256, 3, 4096], P('hour', 'sens'), may hold values from -6 to 6
- pair_first: int32 [2048], P('sens'), may hold values from 0 to 7
- pair_second: int32 [2048], P('sens'), may hold values from 0 to 23
- owners: int32 [2048, 1], P('sens'), may hold values from 0 to 31; in each aligned block of 64 rows (0 to 63, 64 to 127, ...) at most 4 rows name the same one
Outputs:
- stacks: float32 [4096, 9216], P('sens', 'hour')
The draws below stay inside these ranges and needn't reach their ends.
Inputs may be any that keep to these rules, and one draw needn't show every extreme that they name: `owners`: within the 64 pairs of one block no owner appears more than 4 times, and some owner appears exactly 4 times.
All inputs are finite; a program needn't handle non-finite values.
Results may differ from the reference program's by a relative error of at most 0.004.
Values may be sent and summed in bfloat16 or wider, within the bound.
No kernel may reach another device: no remote copies, remote signals or barrier semaphores. Data moves between devices by JAX's collectives and lax.ppermute only.
A program may use at most 128 MiB of HBM per device.

```python
import math
import jax
import jax.numpy as jnp
import numpy as np
from jax import lax

SAMPLES = 4096
PADDED = 8192
NB = 2048
LAGS = 1024
COMPS = 3
S_DEV = 8
PAIRS_DEV = 64
CAP = 4
SENSORS = 256
HOURS = 8
PAIR_ROWS = 2048
SLOTS = 4096
N_SENS = 32


def touch_ends(entries, own_key, smallest, high):
    place = [jax.random.randint(jax.random.fold_in(own_key, axis), (), 0, length) for axis, length in enumerate(entries.shape)]
    longest = entries.shape.index(max(entries.shape))
    neighbour = place[:longest] + [(place[longest] + 1) % entries.shape[longest]] + place[longest + 1:]
    return entries.at[tuple(place)].set(smallest).at[tuple(neighbour)].set(high)


def shard_levels(stream_key, extent, split, smallest, high):
    factor_of, own = 1.0, jax.random.fold_in(stream_key, 6)
    for position, parts in split:
        steps = jnp.exp(jax.random.uniform(jax.random.fold_in(own, position), (parts,), jnp.float32, smallest / len(split), high / len(split)))
        factor_of = factor_of * jnp.repeat(steps, extent[position] // parts).reshape([-1 if axis == position else 1 for axis in range(len(extent))])
    return factor_of


def routed_block(stream_key, own, number, rows, number_of, top, limit, lean):
    order = jax.random.permutation(stream_key, number_of)
    crowded, usual = shares(number_of, rows * top, limit, lean, True), shares(number_of, rows * top, limit, lean, False)
    places = jnp.arange(number_of)

    def named(tallies, rotation):
        used = int((tallies > 0).sum())
        fixed = max(1, used // 4)
        shifted = fixed + (places - fixed + rotation * (used - fixed)) % max(1, number_of - fixed)
        return jnp.zeros((number_of,), jnp.int32).at[order[jnp.where(places < fixed, places, shifted)]].set(jnp.asarray(tallies, jnp.int32))

    tallies = jnp.where(number % 4 == 0, named(crowded, number // 4), named(usual, number - number // 4 - 1))
    mixed = jax.random.permutation(jax.random.fold_in(own, 3), number_of)
    source_of, receiver = mixed[0:number_of // 2 * 2:2], mixed[1:number_of // 2 * 2:2]
    room = jnp.minimum(tallies[source_of] - 1, limit - tallies[receiver]) // 2
    room = jnp.where((source_of == order[0]) | (receiver == order[0]) | (tallies[receiver] == 0), 0, jnp.maximum(room, 0))
    shifted = jax.random.randint(jax.random.fold_in(own, 4), (number_of // 2,), 0, 1 << 20) % (room + 1)
    tallies = tallies.at[source_of].add(-shifted).at[receiver].add(shifted)
    members = jnp.searchsorted(jnp.cumsum(tallies), jnp.arange(rows * top), side="right").astype(jnp.int32)
    table = members.reshape(top, rows).T
    table = table[jax.random.permutation(jax.random.fold_in(own, 1), rows)]
    rotation = jax.random.randint(jax.random.fold_in(own, 2), (rows, 1), 0, top)
    return jnp.take_along_axis(table, (jnp.arange(top)[None, :] + rotation) % top, axis=1)


def shares(count, total, reach, skew, full):
    weights = [(1 << 20) // math.isqrt(standing ** skew) + 1 for standing in range(1, count + 1)]
    largest = reach if full else min(reach, max(-(-total // count), total * weights[0] // sum(weights)))
    least = 1 if total - largest >= count - 1 else 0
    counts, spare = [largest] + [least] * (count - 1), total - largest - least * (count - 1)
    while spare > 0:
        movable = [i for i in range(1, count) if counts[i] < largest] or [i for i in range(1, count) if counts[i] < reach]
        pool, budget = sum([weights[i] for i in movable]), spare
        for i in movable:
            more = min(reach - counts[i], max(1, budget * weights[i] // pool), spare)
            counts[i] = counts[i] + more
            spare = spare - more
    return np.array(counts)


def scatter_about(own_key, dims, scale, limit, split=(), kind=jnp.bfloat16):
    level = shard_levels(own_key, dims, split, -0.22, 0.18) if split else 1.0
    result = jax.random.normal(own_key, dims, jnp.float32) * scale * level
    return jnp.minimum(jnp.maximum(result, -limit), limit).astype(kind)


def setup_inputs(seed: int = 0) -> dict:
    keys = jax.random.split(jax.random.key(seed), 5)
    windows = scatter_about(keys[0], (HOURS, SENSORS, COMPS, SAMPLES), 1.0, 6.0, ((0, 8), (1, 32)))
    pair_first = touch_ends(jax.random.randint(keys[1], (PAIR_ROWS,), 0, S_DEV), jax.random.fold_in(keys[1], 1), 0, S_DEV - 1).astype(jnp.int32)
    pair_second = touch_ends(jax.random.randint(keys[2], (PAIR_ROWS,), 0, 3 * S_DEV), jax.random.fold_in(keys[2], 1), 0, (3 * S_DEV) - 1).astype(jnp.int32)
    owners_keys = jax.random.split(jax.random.fold_in(keys[3], 1), PAIR_ROWS // PAIRS_DEV)
    owners_turns = jax.random.permutation(jax.random.fold_in(keys[3], 3), PAIR_ROWS // PAIRS_DEV)
    owners = jax.vmap(lambda own, number: routed_block(jax.random.fold_in(keys[3], 2), own, number, PAIRS_DEV, N_SENS, 1, CAP, 2))(owners_keys, owners_turns).reshape((PAIR_ROWS, 1))
    return {"windows": windows, "pair_first": pair_first, "pair_second": pair_second, "owners": owners}


def build_tables():
    times = jnp.arange(SAMPLES, dtype=jnp.int32)
    bins = jnp.arange(NB, dtype=jnp.int32) + 1
    phase = times[:, None] * bins[None, :] % PADDED
    angle = phase.astype(jnp.float32) * (2.0 * jnp.pi / PADDED)
    fwd = jnp.concatenate([jnp.cos(angle), -jnp.sin(angle)], axis=1).astype(jnp.bfloat16)
    shifts = jnp.arange(LAGS, dtype=jnp.int32) - LAGS // 2
    phase_back = bins[:, None] * shifts[None, :] % PADDED
    angle_back = phase_back.astype(jnp.float32) * (2.0 * jnp.pi / PADDED)
    inv = jnp.concatenate([jnp.cos(angle_back), -jnp.sin(angle_back)], axis=0).astype(jnp.bfloat16)
    return (fwd, inv)

def whiten(rows, fwd):
    spec = jnp.dot(rows, fwd, preferred_element_type=jnp.float32)
    real_part = spec[:, :NB]
    imag_part = spec[:, NB:]
    power = real_part * real_part + imag_part * imag_part
    level = lax.optimization_barrier(jnp.mean(power, axis=1, keepdims=True))
    scale = 1.0 / jnp.sqrt(power + 0.1 * level + 1e-06)
    return jnp.concatenate([real_part * scale, imag_part * scale], axis=1).astype(jnp.bfloat16)

def correlate(first_spec, second_spec, inv):
    ar = first_spec[..., :NB].astype(jnp.float32)
    ai = first_spec[..., NB:].astype(jnp.float32)
    br = second_spec[..., :NB].astype(jnp.float32)
    bi = second_spec[..., NB:].astype(jnp.float32)
    real_part = ar[:, :, None, :] * br[:, None, :, :] + ai[:, :, None, :] * bi[:, None, :, :]
    imag_part = ar[:, :, None, :] * bi[:, None, :, :] - ai[:, :, None, :] * br[:, None, :, :]
    cross = jnp.concatenate([real_part, imag_part], axis=-1).astype(jnp.bfloat16)
    count = cross.shape[0]
    lagged = jnp.dot(cross.reshape(count * COMPS * COMPS, 2 * NB), inv, preferred_element_type=jnp.float32)
    return lagged.reshape(count, COMPS * COMPS * LAGS)

def reference(windows, pair_first, pair_second, owners):
    fwd, inv = build_tables()

    def one_hour(hour_windows):
        rows = hour_windows.reshape(SENSORS * COMPS, SAMPLES)
        return whiten(rows, fwd).reshape(SENSORS, COMPS, 2 * NB)
    white = lax.map(one_hour, windows)
    rows_index = jnp.arange(PAIR_ROWS, dtype=jnp.int32)
    block = rows_index // PAIRS_DEV
    sensor_a = block * S_DEV + pair_first
    sensor_b = (block + pair_second // S_DEV) % N_SENS * S_DEV + pair_second % S_DEV

    def add_hour(total, hour_white):
        return (total + correlate(hour_white[sensor_a], hour_white[sensor_b], inv), None)
    start = jnp.zeros((PAIR_ROWS, COMPS * COMPS * LAGS), jnp.float32)
    summed, _ = lax.scan(add_hour, start, white)
    stack = summed / jnp.sqrt(jnp.float32(NB * HOURS))
    owner = owners[:, 0].reshape(N_SENS, PAIRS_DEV)
    same = owner[:, :, None] == owner[:, None, :]
    order = jnp.arange(PAIRS_DEV, dtype=jnp.int32)
    earlier = order[None, :] < order[:, None]
    slot = lax.optimization_barrier(jnp.sum((same & earlier[None, :, :]).astype(jnp.int32), axis=2)).reshape(PAIR_ROWS)
    target = owners[:, 0] * (N_SENS * CAP) + block * CAP + slot
    stacks = jnp.zeros((SLOTS, COMPS * COMPS * LAGS), jnp.float32).at[target].set(stack)
    return stacks
```

```python
import jax
import jax.numpy as jnp
import ml_dtypes
import numpy as np
from jax import lax
from jax.experimental import pallas as pl
from jax.experimental.pallas import tpu as pltpu
from jax.sharding import PartitionSpec as P

SAMPLES = 4096
PADDED = 8192
NB = 2048
LAGS = 1024
COMPS = 3
SENSORS = 8
PAIRS = 64
CAP = 4
CHUNKS = 8
SPAN = SAMPLES // CHUNKS
RES = 2 * CHUNKS
BINS = NB // RES
ROWS = COMPS * SENSORS
SLAB = 32
MIB = 1 << 20


def tables():
    k = np.arange(1, RES + 1)
    t2 = np.arange(SPAN)
    q = np.arange(BINS)
    angle = 2 * np.pi * ((k[:, None] * t2[None, :]) % PADDED) / PADDED
    twiddle = np.stack([np.cos(angle), -np.sin(angle)]).astype(np.float32)
    period = PADDED // RES
    angle = 2 * np.pi * ((t2[:, None] * q[None, :]) % period) / period
    cos, sin = np.cos(angle), np.sin(angle)
    exact = np.block([[cos, -sin], [sin, cos]])
    high = exact.astype(ml_dtypes.bfloat16)
    common = np.stack([high, (exact - high.astype(np.float64)).astype(ml_dtypes.bfloat16)])
    bins = (k[:, None] + RES * q[None, :]).reshape(-1)
    shifts = np.arange(LAGS) - LAGS // 2
    angle = 2 * np.pi * ((bins[:, None] * shifts[None, :]) % PADDED) / PADDED
    inverse = np.concatenate([np.cos(angle), -np.sin(angle)]).astype(ml_dtypes.bfloat16)
    return twiddle, common, inverse


def forward(rows, twiddle_ref, common_ref, parts_ref, store):
    chunks = [rows[:, SPAN * i : SPAN * (i + 1)].astype(jnp.float32) for i in range(CHUNKS)]

    def combine(weights):
        total = None
        for weight, chunk in zip(weights, chunks):
            weight = float(weight)
            if abs(weight) < 1e-9:
                continue
            term = chunk if abs(weight - 1) < 1e-9 else -chunk if abs(weight + 1) < 1e-9 else chunk * weight
            total = term if total is None else total + term
        return total

    for k in range(0, CHUNKS + 1):
        angle = 2 * np.pi * ((k * np.arange(CHUNKS)) % RES) / RES
        real_part = combine(np.cos(angle))
        imag_part = combine(-np.sin(angle))
        both = ((RES, 1.0),) if k == 0 else ((CHUNKS, 1.0),) if k == CHUNKS else ((k, 1.0), (RES - k, -1.0))
        for residue, sign in both:
            tr = twiddle_ref[0, residue - 1 : residue, :]
            ti = twiddle_ref[1, residue - 1 : residue, :]
            if imag_part is None:
                yr, yi = real_part * tr, real_part * ti
            elif sign > 0:
                yr, yi = real_part * tr - imag_part * ti, real_part * ti + imag_part * tr
            else:
                yr, yi = real_part * tr + imag_part * ti, real_part * ti - imag_part * tr
            at = pl.ds((residue - 1) * ROWS, ROWS)
            parts_ref[at, :SPAN] = yr
            parts_ref[at, SPAN:] = yi
    both = parts_ref[...]
    high = both.astype(jnp.bfloat16)
    low = (both - high.astype(jnp.float32)).astype(jnp.bfloat16)
    spec = jnp.dot(high, common_ref[0], preferred_element_type=jnp.float32)
    spec = spec + jnp.dot(low, common_ref[0], preferred_element_type=jnp.float32)
    spec = spec + jnp.dot(high, common_ref[1], preferred_element_type=jnp.float32)
    real_part, imag_part = spec[:, :BINS], spec[:, BINS:]
    power = real_part * real_part + imag_part * imag_part
    total = power[:ROWS]
    for k in range(1, RES):
        total = total + power[k * ROWS : (k + 1) * ROWS]
    level = jnp.sum(total, axis=1, keepdims=True) * (1.0 / NB)
    floor = 0.1 * level + 1e-06
    for k in range(RES):
        at = slice(k * ROWS, (k + 1) * ROWS)
        scale = lax.rsqrt(power[at] + floor)
        store(k, jnp.concatenate([real_part[at] * scale, imag_part[at] * scale], axis=1))


def padded(value):
    return jnp.concatenate([value, jnp.zeros((SLAB - ROWS, value.shape[1]), value.dtype)], axis=0).astype(jnp.bfloat16)


def whiten_kernel(rows_ref, twiddle_ref, common_ref, white_ref, parts_ref):
    def store(k, value):
        white_ref[k] = padded(value)

    forward(rows_ref[...], twiddle_ref, common_ref, parts_ref, store)


def pairs_kernel(white_ref, nearer_ref, farther_ref, pick_ref, twiddle_ref, common_ref, inverse_ref, out_ref,
                 parts_ref, all_ref, cross_ref, table_ref, sem):
    load = pltpu.make_async_copy(inverse_ref, table_ref, sem)
    load.start()
    for block, rows_ref in ((1, nearer_ref), (2, farther_ref)):
        def store(k, value, block=block):
            all_ref[k, pl.ds(block * SLAB, SLAB), :] = padded(value)

        forward(rows_ref[...], twiddle_ref, common_ref, parts_ref, store)
    for k in range(RES):
        all_ref[k, pl.ds(0, SLAB), :] = white_ref[k]
        all_ref[k, pl.ds(3 * SLAB, SLAB), :] = jnp.zeros((SLAB, 2 * BINS), jnp.bfloat16)

    def cross(k, carry):
        picked = jnp.dot(pick_ref[...], all_ref[k], preferred_element_type=jnp.float32)
        at_re = pl.ds(pl.multiple_of(k * BINS, BINS), BINS)
        at_im = pl.ds(pl.multiple_of(NB + k * BINS, BINS), BINS)
        for c in range(COMPS):
            first = picked[c * PAIRS : (c + 1) * PAIRS]
            ar, ai = first[:, :BINS], first[:, BINS:]
            for e in range(COMPS):
                second = picked[(COMPS + e) * PAIRS : (COMPS + e + 1) * PAIRS]
                br, bi = second[:, :BINS], second[:, BINS:]
                at = pl.ds((c * COMPS + e) * PAIRS, PAIRS)
                cross_ref[at, at_re] = (ar * br + ai * bi).astype(jnp.bfloat16)
                cross_ref[at, at_im] = (ar * bi - ai * br).astype(jnp.bfloat16)
        return carry

    lax.fori_loop(0, RES, cross, 0)
    load.wait()
    width = 256
    tiles = COMPS * COMPS * LAGS // 128 // out_ref.shape[0]
    for n in range(LAGS // width):
        lagged = jnp.dot(cross_ref[...], table_ref[:, n * width : (n + 1) * width], preferred_element_type=jnp.float32)
        lagged = lagged.astype(jnp.bfloat16)
        for i in range(COMPS * COMPS):
            for half in range(width // 128):
                flat = i * (LAGS // 128) + n * (width // 128) + half
                out_ref[flat // tiles, :, (flat % tiles) * 128 : (flat % tiles + 1) * 128] = lagged[
                    i * PAIRS : (i + 1) * PAIRS, half * 128 : (half + 1) * 128]


def collect_kernel(parts_ref, place_ref, out_ref):
    total = parts_ref[0].astype(jnp.float32)
    for h in range(1, parts_ref.shape[0]):
        total = total + parts_ref[h].astype(jnp.float32)
    total = (total * (1.0 / 128.0)).astype(jnp.bfloat16)
    out_ref[...] = jnp.dot(place_ref[...], total, preferred_element_type=jnp.float32).astype(jnp.bfloat16)


def from_behind(value, axis, steps):
    count = lax.axis_size(axis)
    return lax.ppermute(value, axis, [(source, (source + steps) % count) for source in range(count)])


def shards(windows, pair_first, pair_second, owners):
    twiddle, common, inverse = (jnp.asarray(t) for t in tables())
    hours = lax.axis_size("hour")
    share = COMPS * COMPS * LAGS // hours
    bf16 = jnp.bfloat16
    rows = windows[0].transpose(1, 0, 2).reshape(ROWS, SAMPLES)
    nearer = from_behind(rows, "sens", -1)
    farther = from_behind(rows, "sens", -2)

    comps = jnp.arange(COMPS, dtype=jnp.int32)[:, None] * SENSORS
    pick_first = (comps + pair_first[None, :]).reshape(-1)
    pick_second = (comps + (pair_second // SENSORS * SLAB + pair_second % SENSORS)[None, :]).reshape(-1)
    picks = jnp.concatenate([pick_first, pick_second])
    pick = (picks[:, None] == jnp.arange(4 * SLAB, dtype=jnp.int32)[None, :]).astype(bf16)

    owner = owners[:, 0]
    order = jnp.arange(PAIRS, dtype=jnp.int32)
    same = (owner[:, None] == owner[None, :]) & (order[None, :] < order[:, None])
    target = owner * CAP + jnp.sum(same.astype(jnp.int32), axis=1)
    slots = lax.axis_size("sens") * CAP
    place = (jnp.arange(slots, dtype=jnp.int32)[:, None] == target[None, :]).astype(bf16)

    vmem = pl.BlockSpec(memory_space=pltpu.VMEM)
    white = pl.pallas_call(
        whiten_kernel,
        out_shape=jax.ShapeDtypeStruct((RES, SLAB, 2 * BINS), bf16),
        in_specs=[vmem] * 3,
        out_specs=vmem,
        scratch_shapes=[pltpu.VMEM((RES * ROWS, 2 * SPAN), jnp.float32)],
        compiler_params=pltpu.CompilerParams(vmem_limit_bytes=32 * MIB),
        cost_estimate=pl.CostEstimate(flops=3 * 10**8, bytes_accessed=10**6, transcendentals=0),
        name="whiten",
    )(rows, twiddle, common)
    partial = pl.pallas_call(
        pairs_kernel,
        out_shape=jax.ShapeDtypeStruct((hours, PAIRS, share), bf16),
        in_specs=[vmem] * 6 + [pl.BlockSpec(memory_space=pl.ANY)],
        out_specs=vmem,
        scratch_shapes=[
            pltpu.VMEM((RES * ROWS, 2 * SPAN), jnp.float32),
            pltpu.VMEM((RES, 4 * SLAB, 2 * BINS), bf16),
            pltpu.VMEM((COMPS * COMPS * PAIRS, 2 * NB), bf16),
            pltpu.VMEM((2 * NB, LAGS), bf16),
            pltpu.SemaphoreType.DMA,
        ],
        compiler_params=pltpu.CompilerParams(vmem_limit_bytes=48 * MIB),
        cost_estimate=pl.CostEstimate(flops=6 * 10**9, bytes_accessed=10**7, transcendentals=0),
        name="pairs",
    )(white, nearer, farther, pick, twiddle, common, inverse)
    received = lax.all_to_all(partial, "hour", split_axis=0, concat_axis=0, tiled=True)
    outgoing = pl.pallas_call(
        collect_kernel,
        out_shape=jax.ShapeDtypeStruct((slots, share), bf16),
        in_specs=[vmem] * 2,
        out_specs=vmem,
        compiler_params=pltpu.CompilerParams(vmem_limit_bytes=32 * MIB),
        cost_estimate=pl.CostEstimate(flops=2 * 10**7, bytes_accessed=2 * 10**6, transcendentals=0),
        name="collect",
    )(received, place)
    stacked = lax.all_to_all(outgoing, "sens", split_axis=0, concat_axis=0, tiled=True)
    return stacked.astype(jnp.float32)


def solution(mesh):
    placed = (P("hour", "sens", None, None), P("sens"), P("sens"), P("sens", None))
    return jax.shard_map(
        shards, mesh=mesh, in_specs=placed, out_specs=P("sens", "hour"), check_vma=False
    )
```

```python
import functools

import jax
import jax.numpy as jnp
import ml_dtypes
import numpy as np
from jax import lax
from jax.experimental import pallas as pl
from jax.experimental.pallas import tpu as pltpu
from jax.sharding import PartitionSpec as P

SAMPLES = 4096
PADDED = 8192
NB = 2048
LAGS = 1024
COMPS = 3
SENSORS = 8
PAIRS = 64
CAP = 4
CHUNKS = 8
SPAN = SAMPLES // CHUNKS
RES = 2 * CHUNKS
BINS = NB // RES
ROWS = COMPS * SENSORS
SLAB = 32
HALF = LAGS // 2
TILE = 128
MIB = 1 << 20


def tables():
    k = np.arange(1, RES + 1)
    q = np.arange(BINS)
    twiddles, commons = [], []
    for early in (0.0, 0.5):
        times = np.arange(SPAN) - early
        angle = 2 * np.pi * (k[:, None] * times[None, :] / PADDED)
        twiddles.append(np.stack([np.cos(angle), -np.sin(angle)]).astype(np.float32))
        angle = 2 * np.pi * (times[:, None] * q[None, :] / (PADDED // RES))
        cos, sin = np.cos(angle), np.sin(angle)
        exact = np.block([[cos, -sin], [sin, cos]])
        high = exact.astype(ml_dtypes.bfloat16)
        commons.append(np.stack([high, (exact - high.astype(np.float64)).astype(ml_dtypes.bfloat16)]))
    bins = (k[:, None] + RES * q[None, :]).reshape(-1)
    angle = 2 * np.pi * (bins[:, None] * (np.arange(HALF) + 0.5)[None, :] / PADDED)
    inverse = np.stack([np.cos(angle), np.sin(angle)]).astype(ml_dtypes.bfloat16)
    flip = np.eye(TILE)[::-1].astype(ml_dtypes.bfloat16)
    return np.stack(twiddles), np.stack(commons), inverse, flip


def forward(rows, twiddle_ref, common_ref, parts_ref, store):
    chunks = [rows[:, SPAN * i : SPAN * (i + 1)].astype(jnp.float32) for i in range(CHUNKS)]

    def combine(weights):
        total = None
        for weight, chunk in zip(weights, chunks):
            weight = float(weight)
            if abs(weight) < 1e-9:
                continue
            term = chunk if abs(weight - 1) < 1e-9 else -chunk if abs(weight + 1) < 1e-9 else chunk * weight
            total = term if total is None else total + term
        return total

    for k in range(0, CHUNKS + 1):
        angle = 2 * np.pi * ((k * np.arange(CHUNKS)) % RES) / RES
        real_part = combine(np.cos(angle))
        imag_part = combine(-np.sin(angle))
        both = ((RES, 1.0),) if k == 0 else ((CHUNKS, 1.0),) if k == CHUNKS else ((k, 1.0), (RES - k, -1.0))
        for residue, sign in both:
            tr = twiddle_ref[0, residue - 1 : residue, :]
            ti = twiddle_ref[1, residue - 1 : residue, :]
            if imag_part is None:
                yr, yi = real_part * tr, real_part * ti
            elif sign > 0:
                yr, yi = real_part * tr - imag_part * ti, real_part * ti + imag_part * tr
            else:
                yr, yi = real_part * tr + imag_part * ti, real_part * ti - imag_part * tr
            at = pl.ds((residue - 1) * ROWS, ROWS)
            parts_ref[at, :SPAN] = yr
            parts_ref[at, SPAN:] = yi
    both = parts_ref[...]
    high = both.astype(jnp.bfloat16)
    low = (both - high.astype(jnp.float32)).astype(jnp.bfloat16)
    spec = jnp.dot(high, common_ref[0], preferred_element_type=jnp.float32)
    spec = spec + jnp.dot(low, common_ref[0], preferred_element_type=jnp.float32)
    spec = spec + jnp.dot(high, common_ref[1], preferred_element_type=jnp.float32)
    real_part, imag_part = spec[:, :BINS], spec[:, BINS:]
    power = real_part * real_part + imag_part * imag_part
    total = power[:ROWS]
    for k in range(1, RES):
        total = total + power[k * ROWS : (k + 1) * ROWS]
    level = jnp.sum(total, axis=1, keepdims=True) * (1.0 / NB)
    floor = 0.1 * level + 1e-06
    for k in range(RES):
        at = slice(k * ROWS, (k + 1) * ROWS)
        scale = lax.rsqrt(power[at] + floor)
        store(k, jnp.concatenate([real_part[at] * scale, imag_part[at] * scale], axis=1))


def padded(value):
    return jnp.concatenate([value, jnp.zeros((SLAB - ROWS, value.shape[1]), value.dtype)], axis=0).astype(jnp.bfloat16)


def whiten_kernel(rows_ref, twiddle_ref, common_ref, *refs):
    *white_refs, parts_ref = refs
    for i, white_ref in enumerate(white_refs):
        def store(k, value, white_ref=white_ref):
            white_ref[k] = padded(value)

        forward(rows_ref[...], twiddle_ref.at[i], common_ref.at[i], parts_ref, store)


def pick_kernel(first_ref, second_ref, pick_ref):
    index = lax.broadcasted_iota(jnp.int32, (4 * SLAB, PAIRS), 0)
    first = first_ref[...] + 3 * SLAB
    second = second_ref[...]
    second = second + (second >> 3) * (SLAB - SENSORS)
    columns = [index == at + c * SENSORS for at in (first, second) for c in range(COMPS)]
    spread = jnp.concatenate([c.astype(jnp.float32) for c in columns], axis=1)
    pick_ref[...] = spread.T.astype(jnp.bfloat16)


def cross_kernel(own_ref, turned_ref, nearer_ref, farther_ref, pick_ref, twiddle_ref, common_ref, cross_ref,
                 parts_ref, all_ref):
    def store(k, value):
        all_ref[k, pl.ds(2 * SLAB, SLAB), :] = padded(value)

    forward(farther_ref[...], twiddle_ref.at[0], common_ref.at[0], parts_ref, store)
    for k in range(RES):
        for i, white_ref in ((0, own_ref), (1, nearer_ref), (3, turned_ref)):
            all_ref[k, pl.ds(i * SLAB, SLAB), :] = white_ref[k]

    def cross(k, carry):
        picked = jnp.dot(pick_ref[...], all_ref[k], preferred_element_type=jnp.float32)
        at_re = pl.ds(pl.multiple_of(k * BINS, BINS), BINS)
        at_im = pl.ds(pl.multiple_of(NB + k * BINS, BINS), BINS)
        for c in range(COMPS):
            first = picked[c * PAIRS : (c + 1) * PAIRS]
            ar, ai = first[:, :BINS], first[:, BINS:]
            for e in range(COMPS):
                second = picked[(COMPS + e) * PAIRS : (COMPS + e + 1) * PAIRS]
                br, bi = second[:, :BINS], second[:, BINS:]
                at = c * COMPS + e
                cross_ref[at, :, at_re] = (ar * br + ai * bi).astype(jnp.bfloat16)
                cross_ref[at, :, at_im] = (ar * bi - ai * br).astype(jnp.bfloat16)
        return carry

    lax.fori_loop(0, RES, cross, 0)


def lags_kernel(distances, hour_ref, cross_ref, inverse_ref, flip_ref, *refs):
    *out_refs, tile_ref = refs
    hour = hour_ref[0]
    count = len(distances) + 1
    base = hour ^ distances[0]
    if count == 3:
        base = (base >> 1) * 2
    block = cross_ref[pl.ds(base, count)].reshape(count * PAIRS, 2 * NB)
    even = jnp.dot(block[:, :NB], inverse_ref[0], preferred_element_type=jnp.float32)
    odd = jnp.dot(block[:, NB:], inverse_ref[1], preferred_element_type=jnp.float32)
    after = (even - odd).astype(jnp.bfloat16)
    before = (even + odd).astype(jnp.bfloat16)
    per_comp, per_half = LAGS // TILE, HALF // TILE
    for tile in range(per_half):
        at = slice(tile * TILE, (tile + 1) * TILE)
        turned = jnp.dot(before[:, at], flip_ref[...], preferred_element_type=jnp.float32).astype(jnp.bfloat16)
        for c in range(count):
            of = slice(c * PAIRS, (c + 1) * PAIRS)
            tile_ref[c * per_comp + per_half - 1 - tile] = turned[of]
            tile_ref[c * per_comp + per_half + tile] = after[of, at]
    for distance, out_ref in zip(distances, out_refs):
        tiles = out_ref.shape[1] // TILE
        start = (hour ^ distance) * tiles - base * per_comp
        for u in range(tiles):
            out_ref[:, u * TILE : (u + 1) * TILE] = tile_ref[start + u]


def collect_kernel(place_ref, *refs):
    *parts_refs, out_ref = refs
    total = parts_refs[0][...].astype(jnp.float32)
    for ref in parts_refs[1:]:
        total = total + ref[...].astype(jnp.float32)
    total = (total * (1.0 / 128.0)).astype(jnp.bfloat16)
    out_ref[...] = jnp.dot(place_ref[...], total, preferred_element_type=jnp.float32).astype(jnp.bfloat16)


def from_behind(value, axis, steps):
    count = lax.axis_size(axis)
    return lax.ppermute(value, axis, [(source, (source + steps) % count) for source in range(count)])


def shards(windows, pair_first, pair_second, owners):
    twiddle, common, inverse, flip = (jnp.asarray(t) for t in tables())
    hours = lax.axis_size("hour")
    hour = lax.axis_index("hour").astype(jnp.int32).reshape(1)
    share = COMPS * COMPS * LAGS // hours
    bf16 = jnp.bfloat16
    rows = windows[0].transpose(1, 0, 2).reshape(ROWS, SAMPLES)
    nearer = from_behind(rows, "sens", -1)
    farther = from_behind(rows, "sens", -2)

    owner = owners[:, 0]
    order = jnp.arange(PAIRS, dtype=jnp.int32)
    same = (owner[:, None] == owner[None, :]) & (order[None, :] < order[:, None])
    target = owner * CAP + jnp.sum(same.astype(jnp.int32), axis=1)
    slots = lax.axis_size("sens") * CAP
    place = (jnp.arange(slots, dtype=jnp.int32)[:, None] == target[None, :]).astype(bf16)

    vmem = pl.BlockSpec(memory_space=pltpu.VMEM)
    smem = pl.BlockSpec(memory_space=pltpu.SMEM)
    spectra = jax.ShapeDtypeStruct((RES, SLAB, 2 * BINS), bf16)
    scratch = pltpu.VMEM((RES * ROWS, 2 * SPAN), jnp.float32)

    def whiten(rows, count, name):
        return pl.pallas_call(
            whiten_kernel,
            out_shape=(spectra,) * count,
            in_specs=[vmem] * 3,
            out_specs=(vmem,) * count,
            scratch_shapes=[scratch],
            compiler_params=pltpu.CompilerParams(vmem_limit_bytes=16 * MIB),
            cost_estimate=pl.CostEstimate(flops=10**9 * count, bytes_accessed=10**6, transcendentals=0),
            name=name,
        )(rows, twiddle, common)

    pick = pl.pallas_call(
        pick_kernel,
        out_shape=jax.ShapeDtypeStruct((2 * COMPS * PAIRS, 4 * SLAB), bf16),
        in_specs=[vmem] * 2,
        out_specs=vmem,
        name="pick",
    )(pair_first.reshape(1, PAIRS), pair_second.reshape(1, PAIRS))
    own, turned = whiten(rows, 2, "whiten_own")
    (near,) = whiten(nearer, 1, "whiten_nearer")
    cross = pl.pallas_call(
        cross_kernel,
        out_shape=jax.ShapeDtypeStruct((COMPS * COMPS, PAIRS, 2 * NB), bf16),
        in_specs=[vmem] * 7,
        out_specs=vmem,
        scratch_shapes=[scratch, pltpu.VMEM((RES, 4 * SLAB, 2 * BINS), bf16)],
        compiler_params=pltpu.CompilerParams(vmem_limit_bytes=16 * MIB),
        cost_estimate=pl.CostEstimate(flops=3 * 10**9, bytes_accessed=10**6, transcendentals=0),
        name="cross",
    )(own, turned, near, farther, pick, twiddle, common)

    def lags(distances):
        one = jax.ShapeDtypeStruct((PAIRS, share), bf16)
        return pl.pallas_call(
            functools.partial(lags_kernel, distances),
            out_shape=(one,) * len(distances),
            in_specs=[smem] + [vmem] * 3,
            out_specs=(vmem,) * len(distances),
            scratch_shapes=[pltpu.VMEM((3 * LAGS // TILE, PAIRS, TILE), bf16)],
            compiler_params=pltpu.CompilerParams(vmem_limit_bytes=16 * MIB),
            cost_estimate=pl.CostEstimate(flops=10**9, bytes_accessed=10**6, transcendentals=0),
            name="lags",
        )(hour, cross, inverse, flip)

    parts = []
    for distances in ((6, 7), (4, 5), (2, 3), (1,), (0,)):
        for distance, part in zip(distances, lags(distances)):
            if distance:
                part = lax.ppermute(part, "hour", [(h, h ^ distance) for h in range(hours)])
            parts.append(part)
    outgoing = pl.pallas_call(
        collect_kernel,
        out_shape=jax.ShapeDtypeStruct((slots, share), bf16),
        in_specs=[vmem] * (1 + hours),
        out_specs=vmem,
        compiler_params=pltpu.CompilerParams(vmem_limit_bytes=16 * MIB),
        cost_estimate=pl.CostEstimate(flops=2 * 10**7, bytes_accessed=2 * 10**6, transcendentals=0),
        name="collect",
    )(place, *parts)
    stacked = lax.all_to_all(outgoing, "sens", split_axis=0, concat_axis=0, tiled=True)
    return stacked.astype(jnp.float32)


def solution(mesh):
    placed = (P("hour", "sens", None, None), P("sens"), P("sens"), P("sens", None))
    return jax.shard_map(
        shards, mesh=mesh, in_specs=placed, out_specs=P("sens", "hour"), check_vma=False
    )
```

```python
import functools

import jax
import jax.numpy as jnp
import ml_dtypes
import numpy as np
from jax import lax
from jax.experimental import pallas as pl
from jax.experimental.pallas import tpu as pltpu
from jax.sharding import PartitionSpec as P

SAMPLES = 4096
PADDED = 8192
NB = 2048
LAGS = 1024
COMPS = 3
SENSORS = 8
PAIRS = 64
CAP = 4
CHUNKS = 8
SPAN = SAMPLES // CHUNKS
RES = 2 * CHUNKS
BINS = NB // RES
ROWS = COMPS * SENSORS
SLAB = 32
HALF = LAGS // 2
TILE = 128
MIB = 1 << 20


def tables():
    k = np.arange(1, RES + 1)
    t2 = np.arange(SPAN)
    q = np.arange(BINS)
    angle = 2 * np.pi * ((k[:, None] * t2[None, :]) % PADDED) / PADDED
    twiddle = np.stack([np.cos(angle), -np.sin(angle)]).astype(np.float32)
    period = PADDED // RES
    angle = 2 * np.pi * ((t2[:, None] * q[None, :]) % period) / period
    cos, sin = np.cos(angle), np.sin(angle)
    exact = np.block([[cos, -sin], [sin, cos]])
    high = exact.astype(ml_dtypes.bfloat16)
    common = np.stack([high, (exact - high.astype(np.float64)).astype(ml_dtypes.bfloat16)])
    bins = (k[:, None] + RES * q[None, :]).reshape(-1)
    angle = 2 * np.pi * ((bins[:, None] * np.arange(1, HALF + 1)[None, :]) % PADDED) / PADDED
    cosines = np.zeros((NB, HALF + TILE))
    cosines[:, :HALF] = np.cos(angle)
    cosines[:, -1] = 1.0
    cosines = cosines.astype(ml_dtypes.bfloat16)
    sines = np.sin(angle).astype(ml_dtypes.bfloat16)
    flip = np.eye(TILE)[::-1]
    shift = np.eye(2 * TILE)[:, TILE - 1 : 2 * TILE - 1]
    moves = np.concatenate([flip, shift]).astype(ml_dtypes.bfloat16)
    return twiddle, common, cosines, sines, moves


def forward(rows, twiddle_ref, common_ref, parts_ref, store):
    chunks = [rows[:, SPAN * i : SPAN * (i + 1)].astype(jnp.float32) for i in range(CHUNKS)]

    def combine(weights):
        total = None
        for weight, chunk in zip(weights, chunks):
            weight = float(weight)
            if abs(weight) < 1e-9:
                continue
            term = chunk if abs(weight - 1) < 1e-9 else -chunk if abs(weight + 1) < 1e-9 else chunk * weight
            total = term if total is None else total + term
        return total

    for k in range(0, CHUNKS + 1):
        angle = 2 * np.pi * ((k * np.arange(CHUNKS)) % RES) / RES
        real_part = combine(np.cos(angle))
        imag_part = combine(-np.sin(angle))
        both = ((RES, 1.0),) if k == 0 else ((CHUNKS, 1.0),) if k == CHUNKS else ((k, 1.0), (RES - k, -1.0))
        for residue, sign in both:
            tr = twiddle_ref[0, residue - 1 : residue, :]
            ti = twiddle_ref[1, residue - 1 : residue, :]
            if imag_part is None:
                yr, yi = real_part * tr, real_part * ti
            elif sign > 0:
                yr, yi = real_part * tr - imag_part * ti, real_part * ti + imag_part * tr
            else:
                yr, yi = real_part * tr + imag_part * ti, real_part * ti - imag_part * tr
            at = pl.ds((residue - 1) * ROWS, ROWS)
            parts_ref[at, :SPAN] = yr
            parts_ref[at, SPAN:] = yi
    both = parts_ref[...]
    high = both.astype(jnp.bfloat16)
    low = (both - high.astype(jnp.float32)).astype(jnp.bfloat16)
    spec = jnp.dot(high, common_ref[0], preferred_element_type=jnp.float32)
    spec = spec + jnp.dot(low, common_ref[0], preferred_element_type=jnp.float32)
    spec = spec + jnp.dot(high, common_ref[1], preferred_element_type=jnp.float32)
    real_part, imag_part = spec[:, :BINS], spec[:, BINS:]
    power = real_part * real_part + imag_part * imag_part
    total = power[:ROWS]
    for k in range(1, RES):
        total = total + power[k * ROWS : (k + 1) * ROWS]
    level = jnp.sum(total, axis=1, keepdims=True) * (1.0 / NB)
    floor = 0.1 * level + 1e-06
    for k in range(RES):
        at = slice(k * ROWS, (k + 1) * ROWS)
        scale = lax.rsqrt(power[at] + floor)
        store(k, jnp.concatenate([real_part[at] * scale, imag_part[at] * scale], axis=1))


def padded(value):
    return jnp.concatenate([value, jnp.zeros((SLAB - ROWS, value.shape[1]), value.dtype)], axis=0).astype(jnp.bfloat16)


def one_hot(index, height):
    at = lax.broadcasted_iota(jnp.int32, (height, PAIRS), 0)
    return jnp.concatenate([(at == i).astype(jnp.float32) for i in index], axis=1)


def own_kernel(rows_any, twiddle_any, common_any, first_any, second_any, owner_any,
               white_ref, first_rows_ref, pick_ref, place_ref,
               rows_ref, twiddle_ref, common_ref, first_ref, second_ref, owner_ref, parts_ref, sems):
    sources = (rows_any, twiddle_any, common_any, first_any, second_any, owner_any)
    targets = (rows_ref, twiddle_ref, common_ref, first_ref, second_ref, owner_ref)
    copies = [pltpu.make_async_copy(s, t, sems.at[i]) for i, (s, t) in enumerate(zip(sources, targets))]
    for copy in copies:
        copy.start()
    for copy in copies:
        copy.wait()

    owner = owner_ref[...]
    lanes = jnp.broadcast_to(owner, (PAIRS, PAIRS)).astype(jnp.float32)
    earlier = lax.broadcasted_iota(jnp.int32, (PAIRS, PAIRS), 0) < lax.broadcasted_iota(jnp.int32, (PAIRS, PAIRS), 1)
    same = (lanes == lanes.T) & earlier
    slot = jnp.sum(same.astype(jnp.float32), axis=0, keepdims=True).astype(jnp.int32)
    place_ref[...] = one_hot([owner * CAP + slot], place_ref.shape[0]).astype(jnp.bfloat16)
    second = second_ref[...]
    second = second + (second >> 3) * (SLAB - SENSORS)
    pick_ref[...] = one_hot([second + c * SENSORS for c in range(COMPS)], TILE).T.astype(jnp.bfloat16)
    pick_first = one_hot([first_ref[...] + c * SENSORS for c in range(COMPS)], TILE).T.astype(jnp.bfloat16)[:, :SLAB]

    def store(k, value):
        value = padded(value)
        white_ref[k] = value
        first_rows_ref[k] = jnp.dot(pick_first, value, preferred_element_type=jnp.float32).astype(jnp.bfloat16)

    forward(rows_ref[...], twiddle_ref, common_ref, parts_ref, store)


def nearer_kernel(rows_ref, twiddle_ref, common_ref, white_ref, parts_ref):
    def store(k, value):
        white_ref[k] = padded(value)

    forward(rows_ref[...], twiddle_ref, common_ref, parts_ref, store)


def cross_kernel(first_rows_ref, own_ref, near_ref, farther_ref, pick_ref, twiddle_ref, common_ref, cross_ref,
                 parts_ref, far_ref, second_ref):
    def store(k, value):
        far_ref[k] = padded(value)

    forward(farther_ref[...], twiddle_ref, common_ref, parts_ref, store)
    pick = pick_ref[...]
    group = 16

    def cross(k, carry):
        spectra = jnp.concatenate([own_ref[k], near_ref[k], far_ref[k]], axis=0)
        second_ref[...] = jnp.dot(pick[:, : 3 * SLAB], spectra, preferred_element_type=jnp.float32)
        at_re = pl.ds(pl.multiple_of(k * BINS, BINS), BINS)
        at_im = pl.ds(pl.multiple_of(NB + k * BINS, BINS), BINS)
        for g in range(0, PAIRS, group):
            seconds = [second_ref[e * PAIRS + g : e * PAIRS + g + group, :] for e in range(COMPS)]
            for c in range(COMPS):
                first = first_rows_ref[k, pl.ds(c * PAIRS + g, group), :].astype(jnp.float32)
                ar, ai = first[:, :BINS], first[:, BINS:]
                for e in range(COMPS):
                    br, bi = seconds[e][:, :BINS], seconds[e][:, BINS:]
                    at = c * COMPS + e
                    cross_ref[at, pl.ds(g, group), at_re] = (ar * br + ai * bi).astype(jnp.bfloat16)
                    cross_ref[at, pl.ds(g, group), at_im] = (ar * bi - ai * br).astype(jnp.bfloat16)
        return carry

    lax.fori_loop(0, RES, cross, 0, unroll=2)


def lags_kernel(distances, hour_ref, cross_ref, cosines_ref, sines_ref, moves_ref, *refs):
    *out_refs, tile_ref = refs
    hour = hour_ref[0]
    count = len(distances) + 1
    base = hour ^ distances[0]
    if count == 3:
        base = (base >> 1) * 2
    block = cross_ref[pl.ds(base, count)].reshape(count * PAIRS, 2 * NB)
    even = jnp.dot(block[:, :NB], cosines_ref[...], preferred_element_type=jnp.float32)
    odd = jnp.dot(block[:, NB:], sines_ref[...], preferred_element_type=jnp.float32)
    zero = even[:, HALF:].astype(jnp.bfloat16)
    after = jnp.concatenate([zero, (even[:, :HALF] - odd).astype(jnp.bfloat16)], axis=1)
    before = (even[:, :HALF] + odd).astype(jnp.bfloat16)
    flip, shift = moves_ref[:TILE, :], moves_ref[TILE:, :]
    per_comp, per_half = LAGS // TILE, HALF // TILE
    for tile in range(per_half):
        at = tile * TILE
        turned = jnp.dot(before[:, at : at + TILE], flip, preferred_element_type=jnp.float32).astype(jnp.bfloat16)
        moved = jnp.dot(after[:, at : at + 2 * TILE], shift, preferred_element_type=jnp.float32).astype(jnp.bfloat16)
        for c in range(count):
            of = slice(c * PAIRS, (c + 1) * PAIRS)
            tile_ref[c * per_comp + per_half - 1 - tile] = turned[of]
            tile_ref[c * per_comp + per_half + tile] = moved[of]
    for distance, out_ref in zip(distances, out_refs):
        tiles = out_ref.shape[1] // TILE
        start = (hour ^ distance) * tiles - base * per_comp
        for u in range(tiles):
            out_ref[:, u * TILE : (u + 1) * TILE] = tile_ref[start + u]


def collect_kernel(place_ref, *refs):
    *parts_refs, out_ref = refs
    total = parts_refs[0][...].astype(jnp.float32)
    for ref in parts_refs[1:]:
        total = total + ref[...].astype(jnp.float32)
    total = (total * (1.0 / 128.0)).astype(jnp.bfloat16)
    out_ref[...] = jnp.dot(place_ref[...], total, preferred_element_type=jnp.float32).astype(jnp.bfloat16)


def from_behind(value, axis, steps):
    count = lax.axis_size(axis)
    return lax.ppermute(value, axis, [(source, (source + steps) % count) for source in range(count)])


def shards(windows, pair_first, pair_second, owners):
    twiddle, common, cosines, sines, moves = (jnp.asarray(t) for t in tables())
    hours = lax.axis_size("hour")
    hour = lax.axis_index("hour").astype(jnp.int32).reshape(1)
    share = COMPS * COMPS * LAGS // hours
    slots = lax.axis_size("sens") * CAP
    bf16, f32, i32 = jnp.bfloat16, jnp.float32, jnp.int32
    rows = windows[0].transpose(1, 0, 2).reshape(ROWS, SAMPLES)
    nearer = from_behind(rows, "sens", -1)
    farther = from_behind(rows, "sens", -2)

    vmem = pl.BlockSpec(memory_space=pltpu.VMEM)
    smem = pl.BlockSpec(memory_space=pltpu.SMEM)
    hbm = pl.BlockSpec(memory_space=pltpu.HBM)
    parts_scratch = pltpu.VMEM((RES * ROWS, 2 * SPAN), f32)
    params = pltpu.CompilerParams(vmem_limit_bytes=16 * MIB)

    spectra = jax.ShapeDtypeStruct((RES, SLAB, 2 * BINS), bf16)

    def cost(flops):
        return pl.CostEstimate(flops=flops, bytes_accessed=10**6, transcendentals=0)

    own, first_rows, pick, place = pl.pallas_call(
        own_kernel,
        out_shape=(
            spectra,
            jax.ShapeDtypeStruct((RES, COMPS * PAIRS, 2 * BINS), bf16),
            jax.ShapeDtypeStruct((COMPS * PAIRS, TILE), bf16),
            jax.ShapeDtypeStruct((slots, PAIRS), bf16),
        ),
        in_specs=[hbm] * 6,
        out_specs=(vmem,) * 4,
        scratch_shapes=[
            pltpu.VMEM((ROWS, SAMPLES), bf16),
            pltpu.VMEM(twiddle.shape, f32),
            pltpu.VMEM(common.shape, bf16),
            pltpu.VMEM((1, PAIRS), i32),
            pltpu.VMEM((1, PAIRS), i32),
            pltpu.VMEM((1, PAIRS), i32),
            parts_scratch,
            pltpu.SemaphoreType.DMA((6,)),
        ],
        compiler_params=pltpu.CompilerParams(vmem_limit_bytes=56 * MIB),
        cost_estimate=cost(10**9),
        name="own",
    )(rows, twiddle, common, *(v.reshape(1, PAIRS) for v in (pair_first, pair_second, owners)))
    near = pl.pallas_call(
        nearer_kernel,
        out_shape=spectra,
        in_specs=[vmem] * 3,
        out_specs=vmem,
        scratch_shapes=[parts_scratch],
        compiler_params=params,
        cost_estimate=cost(10**9),
        name="nearer",
    )(nearer, twiddle, common)
    cross = pl.pallas_call(
        cross_kernel,
        out_shape=jax.ShapeDtypeStruct((COMPS * COMPS, PAIRS, 2 * NB), bf16),
        in_specs=[vmem] * 7,
        out_specs=vmem,
        scratch_shapes=[
            parts_scratch,
            pltpu.VMEM((RES, SLAB, 2 * BINS), bf16),
            pltpu.VMEM((COMPS * PAIRS, 2 * BINS), f32),
        ],
        compiler_params=params,
        cost_estimate=cost(3 * 10**9),
        name="cross",
    )(first_rows, own, near, farther, pick, twiddle, common)

    def lags(distances):
        one = jax.ShapeDtypeStruct((PAIRS, share), bf16)
        return pl.pallas_call(
            functools.partial(lags_kernel, distances),
            out_shape=(one,) * len(distances),
            in_specs=[smem] + [vmem] * 4,
            out_specs=(vmem,) * len(distances),
            scratch_shapes=[pltpu.VMEM((3 * LAGS // TILE, PAIRS, TILE), bf16)],
            compiler_params=params,
            cost_estimate=cost(10**9),
            name="lags",
        )(hour, cross, cosines, sines, moves)

    parts = []
    for distances in ((6, 7), (4, 5), (2, 3), (1,), (0,)):
        for distance, part in zip(distances, lags(distances)):
            if distance:
                part = lax.ppermute(part, "hour", [(h, h ^ distance) for h in range(hours)])
            parts.append(part)
    outgoing = pl.pallas_call(
        collect_kernel,
        out_shape=jax.ShapeDtypeStruct((slots, share), bf16),
        in_specs=[vmem] * (1 + hours),
        out_specs=vmem,
        compiler_params=params,
        cost_estimate=cost(2 * 10**7),
        name="collect",
    )(place, *parts)
    stacked = lax.all_to_all(outgoing, "sens", split_axis=0, concat_axis=0, tiled=True)
    return stacked.astype(jnp.float32)


def solution(mesh):
    placed = (P("hour", "sens", None, None), P("sens"), P("sens"), P("sens", None))
    return jax.shard_map(
        shards, mesh=mesh, in_specs=placed, out_specs=P("sens", "hour"), check_vma=False
    )
```

```python
import functools

import jax
import jax.numpy as jnp
import ml_dtypes
import numpy as np
from jax import lax
from jax.experimental import pallas as pl
from jax.experimental.pallas import tpu as pltpu
from jax.sharding import PartitionSpec as P

SAMPLES = 4096
PADDED = 8192
NB = 2048
LAGS = 1024
COMPS = 3
SENSORS = 8
PAIRS = 64
CAP = 4
CHUNKS = 8
SPAN = SAMPLES // CHUNKS
RES = 2 * CHUNKS
BINS = NB // RES
ROWS = COMPS * SENSORS
SLAB = 32
HALF = LAGS // 2
TILE = 128
MIB = 1 << 20


def tables():
    k = np.arange(1, RES + 1)
    t2 = np.arange(SPAN)
    q = np.arange(BINS)
    angle = 2 * np.pi * ((k[:, None] * t2[None, :]) % PADDED) / PADDED
    twiddle = np.stack([np.cos(angle), -np.sin(angle)]).astype(np.float32)
    period = PADDED // RES
    angle = 2 * np.pi * ((t2[:, None] * q[None, :]) % period) / period
    cos, sin = np.cos(angle), np.sin(angle)
    exact = np.block([[cos, -sin], [sin, cos]])
    high = exact.astype(ml_dtypes.bfloat16)
    common = np.stack([high, (exact - high.astype(np.float64)).astype(ml_dtypes.bfloat16)])
    bins = (k[:, None] + RES * q[None, :]).reshape(-1)
    angle = 2 * np.pi * ((bins[:, None] * np.arange(1, HALF + 1)[None, :]) % PADDED) / PADDED
    cosines = np.cos(angle).astype(ml_dtypes.bfloat16)
    sines = np.sin(angle).astype(ml_dtypes.bfloat16)
    flip = np.eye(TILE)[::-1].astype(ml_dtypes.bfloat16)
    return twiddle, common, cosines, sines, flip


def forward(rows, twiddle_ref, common_ref, parts_ref, store):
    chunks = [rows[:, SPAN * i : SPAN * (i + 1)].astype(jnp.float32) for i in range(CHUNKS)]

    def combine(weights):
        total = None
        for weight, chunk in zip(weights, chunks):
            weight = float(weight)
            if abs(weight) < 1e-9:
                continue
            term = chunk if abs(weight - 1) < 1e-9 else -chunk if abs(weight + 1) < 1e-9 else chunk * weight
            total = term if total is None else total + term
        return total

    for k in range(0, CHUNKS + 1):
        angle = 2 * np.pi * ((k * np.arange(CHUNKS)) % RES) / RES
        real_part = combine(np.cos(angle))
        imag_part = combine(-np.sin(angle))
        both = ((RES, 1.0),) if k == 0 else ((CHUNKS, 1.0),) if k == CHUNKS else ((k, 1.0), (RES - k, -1.0))
        for residue, sign in both:
            tr = twiddle_ref[0, residue - 1 : residue, :]
            ti = twiddle_ref[1, residue - 1 : residue, :]
            if imag_part is None:
                yr, yi = real_part * tr, real_part * ti
            elif sign > 0:
                yr, yi = real_part * tr - imag_part * ti, real_part * ti + imag_part * tr
            else:
                yr, yi = real_part * tr + imag_part * ti, real_part * ti - imag_part * tr
            at = pl.ds((residue - 1) * ROWS, ROWS)
            parts_ref[at, :SPAN] = yr
            parts_ref[at, SPAN:] = yi
    both = parts_ref[...]
    high = both.astype(jnp.bfloat16)
    low = (both - high.astype(jnp.float32)).astype(jnp.bfloat16)
    spec = jnp.dot(high, common_ref[0], preferred_element_type=jnp.float32)
    spec = spec + jnp.dot(low, common_ref[0], preferred_element_type=jnp.float32)
    spec = spec + jnp.dot(high, common_ref[1], preferred_element_type=jnp.float32)
    real_part, imag_part = spec[:, :BINS], spec[:, BINS:]
    power = real_part * real_part + imag_part * imag_part
    total = power[:ROWS]
    for k in range(1, RES):
        total = total + power[k * ROWS : (k + 1) * ROWS]
    level = jnp.sum(total, axis=1, keepdims=True) * (1.0 / NB)
    floor = 0.1 * level + 1e-06
    for k in range(RES):
        at = slice(k * ROWS, (k + 1) * ROWS)
        scale = lax.rsqrt(power[at] + floor)
        store(k, jnp.concatenate([real_part[at] * scale, imag_part[at] * scale], axis=1))


def padded(value):
    return jnp.concatenate([value, jnp.zeros((SLAB - ROWS, value.shape[1]), value.dtype)], axis=0).astype(jnp.bfloat16)


def one_hot(index, height):
    at = lax.broadcasted_iota(jnp.int32, (height, PAIRS), 0)
    return jnp.concatenate([(at == i).astype(jnp.float32) for i in index], axis=1)


def own_kernel(rows_any, twiddle_any, common_any, first_any, second_any, owner_any,
               white_ref, first_rows_ref, pick_ref, place_ref,
               rows_ref, twiddle_ref, common_ref, first_ref, second_ref, owner_ref, parts_ref, sems):
    sources = (rows_any, twiddle_any, common_any, first_any, second_any, owner_any)
    targets = (rows_ref, twiddle_ref, common_ref, first_ref, second_ref, owner_ref)
    copies = [pltpu.make_async_copy(s, t, sems.at[i]) for i, (s, t) in enumerate(zip(sources, targets))]
    for copy in copies:
        copy.start()
    for copy in copies:
        copy.wait()

    owner = owner_ref[...]
    lanes = jnp.broadcast_to(owner, (PAIRS, PAIRS)).astype(jnp.float32)
    earlier = lax.broadcasted_iota(jnp.int32, (PAIRS, PAIRS), 0) < lax.broadcasted_iota(jnp.int32, (PAIRS, PAIRS), 1)
    same = (lanes == lanes.T) & earlier
    slot = jnp.sum(same.astype(jnp.float32), axis=0, keepdims=True).astype(jnp.int32)
    place_ref[...] = one_hot([owner * CAP + slot], place_ref.shape[0]).astype(jnp.bfloat16)
    second = second_ref[...]
    second = second + (second >> 3) * (SLAB - SENSORS)
    pick_ref[...] = one_hot([second + c * SENSORS for c in range(COMPS)], TILE).T.astype(jnp.bfloat16)
    pick_first = one_hot([first_ref[...] + c * SENSORS for c in range(COMPS)], TILE).T.astype(jnp.bfloat16)[:, :SLAB]

    def store(k, value):
        value = padded(value)
        white_ref[k] = value
        first_rows_ref[k] = jnp.dot(pick_first, value, preferred_element_type=jnp.float32).astype(jnp.bfloat16)

    forward(rows_ref[...], twiddle_ref, common_ref, parts_ref, store)


def farther_kernel(rows_ref, twiddle_ref, common_ref, white_ref, parts_ref):
    def store(k, value):
        white_ref[k] = padded(value)

    forward(rows_ref[...], twiddle_ref, common_ref, parts_ref, store)


def cross_kernel(odd_ref, first_rows_ref, own_ref, far_ref, sibling_ref, passed_ref, pick_ref, twiddle_ref, common_ref,
                 cross_ref, parts_ref, near_ref, rows_ref, second_ref):
    @pl.when(odd_ref[0] == 0)
    def _():
        rows_ref[...] = sibling_ref[...]

    @pl.when(odd_ref[0] != 0)
    def _():
        rows_ref[...] = passed_ref[...]

    def store(k, value):
        near_ref[k] = padded(value)

    forward(rows_ref[...], twiddle_ref, common_ref, parts_ref, store)
    pick = pick_ref[:, : 3 * SLAB]
    group = 16
    ahead = second_ref.shape[0]

    def cross(step, carry):
        for i in range(ahead):
            k = step * ahead + i
            spectra = jnp.concatenate([own_ref[k], near_ref[k], far_ref[k]], axis=0)
            second_ref[i] = jnp.dot(pick, spectra, preferred_element_type=jnp.float32)
        for i in range(ahead):
            k = step * ahead + i
            at_re = pl.ds(pl.multiple_of(k * BINS, BINS), BINS)
            at_im = pl.ds(pl.multiple_of(NB + k * BINS, BINS), BINS)
            for g in range(0, PAIRS, group):
                seconds = [second_ref[i, e * PAIRS + g : e * PAIRS + g + group, :] for e in range(COMPS)]
                for c in range(COMPS):
                    first = first_rows_ref[k, pl.ds(c * PAIRS + g, group), :].astype(jnp.float32)
                    ar, ai = first[:, :BINS], first[:, BINS:]
                    for e in range(COMPS):
                        br, bi = seconds[e][:, :BINS], seconds[e][:, BINS:]
                        at = c * COMPS + e
                        cross_ref[at, pl.ds(g, group), at_re] = (ar * br + ai * bi).astype(jnp.bfloat16)
                        cross_ref[at, pl.ds(g, group), at_im] = (ar * bi - ai * br).astype(jnp.bfloat16)
        return carry

    lax.fori_loop(0, RES // ahead, cross, 0)


def lags_kernel(distances, hour_ref, cross_ref, cosines_ref, sines_ref, flip_ref, *refs):
    *out_refs, tile_ref = refs
    hour = hour_ref[0]
    count = len(distances) + 1
    base = hour ^ distances[0]
    if count == 3:
        base = (base >> 1) * 2
    block = cross_ref[pl.ds(base, count)].reshape(count * PAIRS, 2 * NB)
    even = jnp.dot(block[:, :NB], cosines_ref[...], preferred_element_type=jnp.float32)
    odd = jnp.dot(block[:, NB:], sines_ref[...], preferred_element_type=jnp.float32)
    zero = jnp.sum(block[:, :NB].astype(jnp.float32), axis=1, keepdims=True)
    later = pltpu.roll(even - odd, 1, axis=1)
    first = lax.broadcasted_iota(jnp.int32, later.shape, 1) == 0
    after = jnp.where(first, zero, later).astype(jnp.bfloat16)
    before = (even + odd).astype(jnp.bfloat16)
    per_comp, per_half = LAGS // TILE, HALF // TILE
    for tile in range(per_half):
        at = tile * TILE
        turned = jnp.dot(before[:, at : at + TILE], flip_ref[...], preferred_element_type=jnp.float32)
        turned = turned.astype(jnp.bfloat16)
        for c in range(count):
            of = slice(c * PAIRS, (c + 1) * PAIRS)
            tile_ref[c * per_comp + per_half - 1 - tile] = turned[of]
            tile_ref[c * per_comp + per_half + tile] = after[of, at : at + TILE]
    for distance, out_ref in zip(distances, out_refs):
        tiles = out_ref.shape[1] // TILE
        start = (hour ^ distance) * tiles - base * per_comp
        for u in range(tiles):
            out_ref[:, u * TILE : (u + 1) * TILE] = tile_ref[start + u]


def collect_kernel(place_ref, *refs):
    *parts_refs, out_ref = refs
    total = parts_refs[0][...].astype(jnp.float32)
    for ref in parts_refs[1:]:
        total = total + ref[...].astype(jnp.float32)
    total = (total * (1.0 / 128.0)).astype(jnp.bfloat16)
    out_ref[...] = jnp.dot(place_ref[...], total, preferred_element_type=jnp.float32).astype(jnp.bfloat16)


def shards(windows, pair_first, pair_second, owners):
    twiddle, common, cosines, sines, flip = (jnp.asarray(t) for t in tables())
    hours = lax.axis_size("hour")
    hour = lax.axis_index("hour").astype(jnp.int32).reshape(1)
    share = COMPS * COMPS * LAGS // hours
    slots = lax.axis_size("sens") * CAP
    bf16, f32, i32 = jnp.bfloat16, jnp.float32, jnp.int32
    rows = windows[0].transpose(1, 0, 2).reshape(ROWS, SAMPLES)
    sens = lax.axis_size("sens")
    swap = [(s, s ^ 1) for s in range(sens)]
    farther = lax.ppermute(rows, "sens", [(s, (s - 2) % sens) for s in range(sens)])
    sibling = lax.ppermute(rows, "sens", swap)
    odd = (lax.axis_index("sens") & 1).astype(jnp.int32).reshape(1)

    vmem = pl.BlockSpec(memory_space=pltpu.VMEM)
    smem = pl.BlockSpec(memory_space=pltpu.SMEM)
    hbm = pl.BlockSpec(memory_space=pltpu.HBM)
    parts_scratch = pltpu.VMEM((RES * ROWS, 2 * SPAN), f32)
    params = pltpu.CompilerParams(vmem_limit_bytes=16 * MIB)

    spectra = jax.ShapeDtypeStruct((RES, SLAB, 2 * BINS), bf16)

    def cost(flops):
        return pl.CostEstimate(flops=flops, bytes_accessed=10**6, transcendentals=0)

    own, first_rows, pick, place = pl.pallas_call(
        own_kernel,
        out_shape=(
            spectra,
            jax.ShapeDtypeStruct((RES, COMPS * PAIRS, 2 * BINS), bf16),
            jax.ShapeDtypeStruct((COMPS * PAIRS, TILE), bf16),
            jax.ShapeDtypeStruct((slots, PAIRS), bf16),
        ),
        in_specs=[hbm] * 6,
        out_specs=(vmem,) * 4,
        scratch_shapes=[
            pltpu.VMEM((ROWS, SAMPLES), bf16),
            pltpu.VMEM(twiddle.shape, f32),
            pltpu.VMEM(common.shape, bf16),
            pltpu.VMEM((1, PAIRS), i32),
            pltpu.VMEM((1, PAIRS), i32),
            pltpu.VMEM((1, PAIRS), i32),
            parts_scratch,
            pltpu.SemaphoreType.DMA((6,)),
        ],
        compiler_params=pltpu.CompilerParams(vmem_limit_bytes=56 * MIB),
        cost_estimate=cost(10**9),
        name="own",
    )(rows, twiddle, common, *(v.reshape(1, PAIRS) for v in (pair_first, pair_second, owners)))
    farther, pick = lax.optimization_barrier((farther, pick))
    passed = lax.ppermute(farther, "sens", swap)
    far = pl.pallas_call(
        farther_kernel,
        out_shape=spectra,
        in_specs=[vmem] * 3,
        out_specs=vmem,
        scratch_shapes=[parts_scratch],
        compiler_params=params,
        cost_estimate=cost(10**9),
        name="farther",
    )(farther, twiddle, common)
    cross = pl.pallas_call(
        cross_kernel,
        out_shape=jax.ShapeDtypeStruct((COMPS * COMPS, PAIRS, 2 * NB), bf16),
        in_specs=[smem] + [vmem] * 8,
        out_specs=vmem,
        scratch_shapes=[
            parts_scratch,
            pltpu.VMEM((RES, SLAB, 2 * BINS), bf16),
            pltpu.VMEM((ROWS, SAMPLES), bf16),
            pltpu.VMEM((4, COMPS * PAIRS, 2 * BINS), f32),
        ],
        compiler_params=params,
        cost_estimate=cost(3 * 10**9),
        name="cross",
    )(odd, first_rows, own, far, sibling, passed, pick, twiddle, common)

    def lags(distances):
        one = jax.ShapeDtypeStruct((PAIRS, share), bf16)
        return pl.pallas_call(
            functools.partial(lags_kernel, distances),
            out_shape=(one,) * len(distances),
            in_specs=[smem] + [vmem] * 4,
            out_specs=(vmem,) * len(distances),
            scratch_shapes=[pltpu.VMEM((3 * LAGS // TILE, PAIRS, TILE), bf16)],
            compiler_params=params,
            cost_estimate=cost(10**9),
            name="lags",
        )(hour, cross, cosines, sines, flip)

    parts = []
    for distances in ((6, 7), (4, 5), (2, 3), (1,), (0,)):
        for distance, part in zip(distances, lags(distances)):
            if distance:
                part = lax.ppermute(part, "hour", [(h, h ^ distance) for h in range(hours)])
            parts.append(part)
    outgoing = pl.pallas_call(
        collect_kernel,
        out_shape=jax.ShapeDtypeStruct((slots, share), bf16),
        in_specs=[vmem] * (1 + hours),
        out_specs=vmem,
        compiler_params=params,
        cost_estimate=cost(2 * 10**7),
        name="collect",
    )(place, *parts)
    stacked = lax.all_to_all(outgoing, "sens", split_axis=0, concat_axis=0, tiled=True)
    return stacked.astype(jnp.float32)


def solution(mesh):
    placed = (P("hour", "sens", None, None), P("sens"), P("sens"), P("sens", None))
    return jax.shard_map(
        shards, mesh=mesh, in_specs=placed, out_specs=P("sens", "hour"), check_vma=False
    )
```

```python
import functools

import jax
import jax.numpy as jnp
import ml_dtypes
import numpy as np
from jax import lax
from jax.experimental import pallas as pl
from jax.experimental.pallas import tpu as pltpu
from jax.sharding import PartitionSpec as P

SAMPLES = 4096
PADDED = 8192
NB = 2048
LAGS = 1024
COMPS = 3
SENSORS = 8
PAIRS = 64
CAP = 4
CHUNKS = 8
SPAN = SAMPLES // CHUNKS
RES = 2 * CHUNKS
BINS = NB // RES
ROWS = COMPS * SENSORS
SLAB = 32
HALF = LAGS // 2
PICKED = COMPS * PAIRS
TILE = 128
MIB = 1 << 20


def tables():
    k = np.arange(1, RES + 1)
    t2 = np.arange(SPAN)
    q = np.arange(BINS)
    angle = 2 * np.pi * ((k[:, None] * t2[None, :]) % PADDED) / PADDED
    twiddle = np.stack([np.cos(angle), -np.sin(angle)]).astype(np.float32)
    period = PADDED // RES
    angle = 2 * np.pi * ((t2[:, None] * q[None, :]) % period) / period
    cos, sin = np.cos(angle), np.sin(angle)
    exact = np.block([[cos, -sin], [sin, cos]])
    high = exact.astype(ml_dtypes.bfloat16)
    common = np.stack([high, (exact - high.astype(np.float64)).astype(ml_dtypes.bfloat16)])
    bins = (k[:, None] + RES * q[None, :]).reshape(-1)
    angle = 2 * np.pi * ((bins[:, None] * np.arange(1, HALF + 1)[None, :]) % PADDED) / PADDED
    cosines = np.cos(angle).astype(ml_dtypes.bfloat16)
    sines = np.sin(angle).astype(ml_dtypes.bfloat16)
    flip = np.eye(TILE)[::-1].astype(ml_dtypes.bfloat16)
    return twiddle, common, cosines, sines, flip


def forward(rows, twiddle_ref, common_ref, parts_ref, store):
    chunks = [rows[:, SPAN * i : SPAN * (i + 1)].astype(jnp.float32) for i in range(CHUNKS)]

    def combine(weights):
        total = None
        for weight, chunk in zip(weights, chunks):
            weight = float(weight)
            if abs(weight) < 1e-9:
                continue
            term = chunk if abs(weight - 1) < 1e-9 else -chunk if abs(weight + 1) < 1e-9 else chunk * weight
            total = term if total is None else total + term
        return total

    for k in range(0, CHUNKS + 1):
        angle = 2 * np.pi * ((k * np.arange(CHUNKS)) % RES) / RES
        real_part = combine(np.cos(angle))
        imag_part = combine(-np.sin(angle))
        both = ((RES, 1.0),) if k == 0 else ((CHUNKS, 1.0),) if k == CHUNKS else ((k, 1.0), (RES - k, -1.0))
        for residue, sign in both:
            tr = twiddle_ref[0, residue - 1 : residue, :]
            ti = twiddle_ref[1, residue - 1 : residue, :]
            if imag_part is None:
                yr, yi = real_part * tr, real_part * ti
            elif sign > 0:
                yr, yi = real_part * tr - imag_part * ti, real_part * ti + imag_part * tr
            else:
                yr, yi = real_part * tr + imag_part * ti, real_part * ti - imag_part * tr
            at = pl.ds((residue - 1) * ROWS, ROWS)
            parts_ref[at, :SPAN] = yr
            parts_ref[at, SPAN:] = yi
    both = parts_ref[...]
    high = both.astype(jnp.bfloat16)
    low = (both - high.astype(jnp.float32)).astype(jnp.bfloat16)
    spec = jnp.dot(high, common_ref[0], preferred_element_type=jnp.float32)
    spec = spec + jnp.dot(low, common_ref[0], preferred_element_type=jnp.float32)
    spec = spec + jnp.dot(high, common_ref[1], preferred_element_type=jnp.float32)
    real_part, imag_part = spec[:, :BINS], spec[:, BINS:]
    power = real_part * real_part + imag_part * imag_part
    total = power[:ROWS]
    for k in range(1, RES):
        total = total + power[k * ROWS : (k + 1) * ROWS]
    level = jnp.sum(total, axis=1, keepdims=True) * (1.0 / NB)
    floor = 0.1 * level + 1e-06
    for k in range(RES):
        at = slice(k * ROWS, (k + 1) * ROWS)
        scale = lax.rsqrt(power[at] + floor)
        store(k, jnp.concatenate([real_part[at] * scale, imag_part[at] * scale], axis=1))


def padded(value):
    return jnp.concatenate([value, jnp.zeros((SLAB - ROWS, value.shape[1]), value.dtype)], axis=0).astype(jnp.bfloat16)


def one_hot(index, height):
    at = lax.broadcasted_iota(jnp.int32, (height, PAIRS), 0)
    return jnp.concatenate([(at == i).astype(jnp.float32) for i in index], axis=1)


def own_kernel(rows_any, twiddle_any, common_any, first_any, second_any, owner_any,
               kept_ref, place_ref,
               rows_ref, twiddle_ref, common_ref, first_ref, second_ref, owner_ref, parts_ref, sems):
    sources = (rows_any, twiddle_any, common_any, first_any, second_any, owner_any)
    targets = (rows_ref, twiddle_ref, common_ref, first_ref, second_ref, owner_ref)
    copies = [pltpu.make_async_copy(s, t, sems.at[i]) for i, (s, t) in enumerate(zip(sources, targets))]
    for copy in copies:
        copy.start()
    for copy in copies:
        copy.wait()

    owner = owner_ref[...]
    lanes = jnp.broadcast_to(owner, (PAIRS, PAIRS)).astype(jnp.float32)
    earlier = lax.broadcasted_iota(jnp.int32, (PAIRS, PAIRS), 0) < lax.broadcasted_iota(jnp.int32, (PAIRS, PAIRS), 1)
    same = (lanes == lanes.T) & earlier
    slot = jnp.sum(same.astype(jnp.float32), axis=0, keepdims=True).astype(jnp.int32)
    place_ref[...] = one_hot([owner * CAP + slot], place_ref.shape[0]).astype(jnp.bfloat16)
    second = second_ref[...]
    second = second + (second >> 3) * (SLAB - SENSORS)
    kept_ref[RES] = jnp.zeros(kept_ref.shape[1:], jnp.bfloat16)
    kept_ref[RES, pl.ds(0, PICKED), pl.ds(0, TILE)] = one_hot([second + c * SENSORS for c in range(COMPS)], TILE).T.astype(jnp.bfloat16)
    pick_first = one_hot([first_ref[...] + c * SENSORS for c in range(COMPS)], TILE).T.astype(jnp.bfloat16)[:, :SLAB]

    def store(k, value):
        value = padded(value)
        kept_ref[k, pl.ds(PICKED, SLAB), :] = value
        first = jnp.dot(pick_first, value, preferred_element_type=jnp.float32)
        kept_ref[k, pl.ds(0, PICKED), :] = first.astype(jnp.bfloat16)

    forward(rows_ref[...], twiddle_ref, common_ref, parts_ref, store)


def farther_kernel(rows_ref, twiddle_ref, common_ref, white_ref, parts_ref):
    def store(k, value):
        white_ref[k] = padded(value)

    forward(rows_ref[...], twiddle_ref, common_ref, parts_ref, store)


def shares(distances, hour, kept_ref, second_rows_ref, cosines_ref, sines_ref, flip_ref, out_refs, cross_ref, tile_ref):
    count = cross_ref.shape[0]
    base = ((hour ^ distances[0]) >> 2) * (count - 1)
    comps = [base + i for i in range(count)]
    firsts = [lax.div(i, COMPS) for i in comps]
    seconds = [i - f * COMPS for i, f in zip(comps, firsts)]
    group = 16

    def cross(k, carry):
        at_re = pl.ds(pl.multiple_of(k * BINS, BINS), BINS)
        at_im = pl.ds(pl.multiple_of(NB + k * BINS, BINS), BINS)
        for i in range(count):
            for g in range(0, PAIRS, group):
                first_at = pl.ds(pl.multiple_of(firsts[i] * PAIRS + g, group), group)
                second_at = pl.ds(pl.multiple_of(seconds[i] * PAIRS + g, group), group)
                first = kept_ref[k, first_at, :].astype(jnp.float32)
                second = second_rows_ref[k, second_at, :].astype(jnp.float32)
                ar, ai = first[:, :BINS], first[:, BINS:]
                br, bi = second[:, :BINS], second[:, BINS:]
                cross_ref[i, pl.ds(g, group), at_re] = (ar * br + ai * bi).astype(jnp.bfloat16)
                cross_ref[i, pl.ds(g, group), at_im] = (ar * bi - ai * br).astype(jnp.bfloat16)
        return carry

    lax.fori_loop(0, RES, cross, 0)
    block = cross_ref[...].reshape(count * PAIRS, 2 * NB)
    even = jnp.dot(block[:, :NB], cosines_ref[...], preferred_element_type=jnp.float32)
    odd = jnp.dot(block[:, NB:], sines_ref[...], preferred_element_type=jnp.float32)
    zero = jnp.sum(block[:, :NB].astype(jnp.float32), axis=1, keepdims=True)
    later = pltpu.roll(even - odd, 1, axis=1)
    start = lax.broadcasted_iota(jnp.int32, later.shape, 1) == 0
    after = jnp.where(start, zero, later).astype(jnp.bfloat16)
    before = (even + odd).astype(jnp.bfloat16)
    per_comp, per_half = LAGS // TILE, HALF // TILE
    for tile in range(per_half):
        at = tile * TILE
        turned = jnp.dot(before[:, at : at + TILE], flip_ref[...], preferred_element_type=jnp.float32)
        turned = turned.astype(jnp.bfloat16)
        for c in range(count):
            of = slice(c * PAIRS, (c + 1) * PAIRS)
            tile_ref[c * per_comp + per_half - 1 - tile] = turned[of]
            tile_ref[c * per_comp + per_half + tile] = after[of, at : at + TILE]
    for distance, out_ref in zip(distances, out_refs):
        tiles = out_ref.shape[1] // TILE
        begin = (hour ^ distance) * tiles - base * per_comp
        for u in range(tiles):
            out_ref[:, u * TILE : (u + 1) * TILE] = tile_ref[begin + u]


def across_kernel(distances, where_ref, kept_ref, far_ref, sibling_ref, passed_ref, twiddle_ref, common_ref,
                  cosines_ref, sines_ref, flip_ref, *refs):
    *out_refs, second_rows_ref, cross_ref, tile_ref, parts_ref, near_ref, rows_ref = refs

    @pl.when(where_ref[1] == 0)
    def _():
        rows_ref[...] = sibling_ref[...]

    @pl.when(where_ref[1] != 0)
    def _():
        rows_ref[...] = passed_ref[...]

    def store(k, value):
        near_ref[k] = padded(value)

    forward(rows_ref[...], twiddle_ref, common_ref, parts_ref, store)
    pick = kept_ref[RES, pl.ds(0, PICKED), pl.ds(0, TILE)][:, : 3 * SLAB]
    for k in range(RES):
        spectra = jnp.concatenate([kept_ref[k, pl.ds(PICKED, SLAB), :], near_ref[k], far_ref[k]], axis=0)
        second = jnp.dot(pick, spectra, preferred_element_type=jnp.float32)
        second_rows_ref[k] = second.astype(jnp.bfloat16)
    shares(distances, where_ref[0], kept_ref, second_rows_ref, cosines_ref, sines_ref, flip_ref, out_refs, cross_ref,
           tile_ref)


def along_kernel(distances, where_ref, kept_ref, second_rows_ref, cosines_ref, sines_ref, flip_ref, *refs):
    *out_refs, cross_ref, tile_ref = refs
    shares(distances, where_ref[0], kept_ref, second_rows_ref, cosines_ref, sines_ref, flip_ref, out_refs, cross_ref,
           tile_ref)


def collect_kernel(place_ref, *refs):
    *parts_refs, out_ref = refs
    total = parts_refs[0][...].astype(jnp.float32)
    for ref in parts_refs[1:]:
        total = total + ref[...].astype(jnp.float32)
    total = (total * (1.0 / 128.0)).astype(jnp.bfloat16)
    out_ref[...] = jnp.dot(place_ref[...], total, preferred_element_type=jnp.float32).astype(jnp.bfloat16)


def shards(windows, pair_first, pair_second, owners):
    twiddle, common, cosines, sines, flip = (jnp.asarray(t) for t in tables())
    hours = lax.axis_size("hour")
    share = COMPS * COMPS * LAGS // hours
    slots = lax.axis_size("sens") * CAP
    bf16, f32, i32 = jnp.bfloat16, jnp.float32, jnp.int32
    rows = windows[0].transpose(1, 0, 2).reshape(ROWS, SAMPLES)
    sens = lax.axis_size("sens")
    swap = [(s, s ^ 1) for s in range(sens)]
    farther = lax.ppermute(rows, "sens", [(s, (s - 2) % sens) for s in range(sens)])
    sibling = lax.ppermute(rows, "sens", swap)
    where = jnp.stack([lax.axis_index("hour"), lax.axis_index("sens") & 1]).astype(jnp.int32)

    vmem = pl.BlockSpec(memory_space=pltpu.VMEM)
    smem = pl.BlockSpec(memory_space=pltpu.SMEM)
    hbm = pl.BlockSpec(memory_space=pltpu.HBM)
    parts_scratch = pltpu.VMEM((RES * ROWS, 2 * SPAN), f32)
    params = pltpu.CompilerParams(vmem_limit_bytes=16 * MIB)

    spectra = jax.ShapeDtypeStruct((RES, SLAB, 2 * BINS), bf16)

    def cost(flops):
        return pl.CostEstimate(flops=flops, bytes_accessed=10**6, transcendentals=0)

    kept, place = pl.pallas_call(
        own_kernel,
        out_shape=(
            pltpu.VMEM((RES + 1, PICKED + SLAB, 2 * BINS), bf16),
            pltpu.VMEM((slots, PAIRS), bf16),
        ),
        in_specs=[hbm] * 6,
        out_specs=(vmem,) * 2,
        scratch_shapes=[
            pltpu.VMEM((ROWS, SAMPLES), bf16),
            pltpu.VMEM(twiddle.shape, f32),
            pltpu.VMEM(common.shape, bf16),
            pltpu.VMEM((1, PAIRS), i32),
            pltpu.VMEM((1, PAIRS), i32),
            pltpu.VMEM((1, PAIRS), i32),
            parts_scratch,
            pltpu.SemaphoreType.DMA((6,)),
        ],
        compiler_params=pltpu.CompilerParams(vmem_limit_bytes=56 * MIB),
        cost_estimate=cost(10**9),
        name="own",
    )(rows, twiddle, common, *(v.reshape(1, PAIRS) for v in (pair_first, pair_second, owners)))
    farther, place = lax.optimization_barrier((farther, place))
    passed = lax.ppermute(farther, "sens", swap)
    far = pl.pallas_call(
        farther_kernel,
        out_shape=spectra,
        in_specs=[vmem] * 3,
        out_specs=vmem,
        scratch_shapes=[parts_scratch],
        compiler_params=params,
        cost_estimate=cost(10**9),
        name="farther",
    )(farther, twiddle, common)
    one = jax.ShapeDtypeStruct((PAIRS, share), bf16)
    half = COMPS * COMPS // 2 + 1
    shares_scratch = [pltpu.VMEM((half, PAIRS, 2 * NB), bf16), pltpu.VMEM((half * LAGS // TILE, PAIRS, TILE), bf16)]
    big = pltpu.CompilerParams(vmem_limit_bytes=24 * MIB)
    other, same = (7, 6, 5, 4), (3, 2, 1, 0)
    *across, second_rows = pl.pallas_call(
        functools.partial(across_kernel, other),
        out_shape=(one,) * 4 + (jax.ShapeDtypeStruct((RES, PICKED, 2 * BINS), bf16),),
        in_specs=[smem] + [vmem] * 9,
        out_specs=(vmem,) * 5,
        scratch_shapes=shares_scratch + [parts_scratch, pltpu.VMEM((RES, SLAB, 2 * BINS), bf16), pltpu.VMEM((ROWS, SAMPLES), bf16)],
        compiler_params=big,
        cost_estimate=cost(3 * 10**9),
        name="across",
    )(where, kept, far, sibling, passed, twiddle, common, cosines, sines, flip)
    along = pl.pallas_call(
        functools.partial(along_kernel, same),
        out_shape=(one,) * 4,
        in_specs=[smem] + [vmem] * 5,
        out_specs=(vmem,) * 4,
        scratch_shapes=shares_scratch,
        compiler_params=big,
        cost_estimate=cost(3 * 10**9),
        name="along",
    )(where, kept, second_rows, cosines, sines, flip)
    parts = []
    for distance, part in zip(other + same, [*across, *along]):
        if distance:
            part = lax.ppermute(part, "hour", [(h, h ^ distance) for h in range(hours)])
        parts.append(part)
    outgoing = pl.pallas_call(
        collect_kernel,
        out_shape=jax.ShapeDtypeStruct((slots, share), bf16),
        in_specs=[vmem] * (1 + hours),
        out_specs=vmem,
        compiler_params=params,
        cost_estimate=cost(2 * 10**7),
        name="collect",
    )(place, *parts)
    stacked = lax.all_to_all(outgoing, "sens", split_axis=0, concat_axis=0, tiled=True)
    return stacked.astype(jnp.float32)


def solution(mesh):
    placed = (P("hour", "sens", None, None), P("sens"), P("sens"), P("sens", None))
    return jax.shard_map(
        shards, mesh=mesh, in_specs=placed, out_specs=P("sens", "hour"), check_vma=False
    )
```

```python
import functools

import jax
import jax.numpy as jnp
import ml_dtypes
import numpy as np
from jax import lax
from jax.experimental import pallas as pl
from jax.experimental.pallas import tpu as pltpu
from jax.sharding import PartitionSpec as P

SAMPLES = 4096
PADDED = 8192
NB = 2048
LAGS = 1024
COMPS = 3
SENSORS = 8
PAIRS = 64
CAP = 4
CHUNKS = 8
SPAN = SAMPLES // CHUNKS
RES = 2 * CHUNKS
BINS = NB // RES
ROWS = COMPS * SENSORS
SLAB = 32
HALF = LAGS // 2
PICKED = COMPS * PAIRS
TILE = 128
MIB = 1 << 20


def tables():
    k = np.arange(1, RES + 1)
    t2 = np.arange(SPAN)
    q = np.arange(BINS)
    angle = 2 * np.pi * ((k[:, None] * t2[None, :]) % PADDED) / PADDED
    twiddle = np.stack([np.cos(angle), -np.sin(angle)]).astype(np.float32)
    period = PADDED // RES
    angle = 2 * np.pi * ((t2[:, None] * q[None, :]) % period) / period
    cos, sin = np.cos(angle), np.sin(angle)
    exact = np.block([[cos, -sin], [sin, cos]])
    high = exact.astype(ml_dtypes.bfloat16)
    common = np.stack([high, (exact - high.astype(np.float64)).astype(ml_dtypes.bfloat16)])
    bins = (k[:, None] + RES * q[None, :]).reshape(-1)
    angle = 2 * np.pi * ((bins[:, None] * np.arange(1, HALF + 1)[None, :]) % PADDED) / PADDED
    cosines = np.cos(angle).astype(ml_dtypes.bfloat16)
    sines = np.sin(angle).astype(ml_dtypes.bfloat16)
    flip = np.eye(TILE)[::-1].astype(ml_dtypes.bfloat16)
    return twiddle, common, cosines, sines, flip


def forward(rows, twiddle_ref, common_ref, parts_ref, store):
    chunks = [rows[:, SPAN * i : SPAN * (i + 1)].astype(jnp.float32) for i in range(CHUNKS)]

    def combine(weights):
        total = None
        for weight, chunk in zip(weights, chunks):
            weight = float(weight)
            if abs(weight) < 1e-9:
                continue
            term = chunk if abs(weight - 1) < 1e-9 else -chunk if abs(weight + 1) < 1e-9 else chunk * weight
            total = term if total is None else total + term
        return total

    for k in range(0, CHUNKS + 1):
        angle = 2 * np.pi * ((k * np.arange(CHUNKS)) % RES) / RES
        real_part = combine(np.cos(angle))
        imag_part = combine(-np.sin(angle))
        both = ((RES, 1.0),) if k == 0 else ((CHUNKS, 1.0),) if k == CHUNKS else ((k, 1.0), (RES - k, -1.0))
        for residue, sign in both:
            tr = twiddle_ref[0, residue - 1 : residue, :]
            ti = twiddle_ref[1, residue - 1 : residue, :]
            if imag_part is None:
                yr, yi = real_part * tr, real_part * ti
            elif sign > 0:
                yr, yi = real_part * tr - imag_part * ti, real_part * ti + imag_part * tr
            else:
                yr, yi = real_part * tr + imag_part * ti, real_part * ti - imag_part * tr
            at = pl.ds((residue - 1) * ROWS, ROWS)
            parts_ref[at, :SPAN] = yr
            parts_ref[at, SPAN:] = yi
    both = parts_ref[...]
    high = both.astype(jnp.bfloat16)
    low = (both - high.astype(jnp.float32)).astype(jnp.bfloat16)
    spec = jnp.dot(high, common_ref[0], preferred_element_type=jnp.float32)
    spec = spec + jnp.dot(low, common_ref[0], preferred_element_type=jnp.float32)
    spec = spec + jnp.dot(high, common_ref[1], preferred_element_type=jnp.float32)
    real_part, imag_part = spec[:, :BINS], spec[:, BINS:]
    power = real_part * real_part + imag_part * imag_part
    total = power[:ROWS]
    for k in range(1, RES):
        total = total + power[k * ROWS : (k + 1) * ROWS]
    level = jnp.sum(total, axis=1, keepdims=True) * (1.0 / NB)
    floor = 0.1 * level + 1e-06
    for k in range(RES):
        at = slice(k * ROWS, (k + 1) * ROWS)
        scale = lax.rsqrt(power[at] + floor)
        store(k, jnp.concatenate([real_part[at] * scale, imag_part[at] * scale], axis=1))


def padded(value):
    return jnp.concatenate([value, jnp.zeros((SLAB - ROWS, value.shape[1]), value.dtype)], axis=0).astype(jnp.bfloat16)


def one_hot(index, height):
    at = lax.broadcasted_iota(jnp.int32, (height, PAIRS), 0)
    return jnp.concatenate([(at == i).astype(jnp.float32) for i in index], axis=1)


def own_kernel(rows_any, twiddle_any, common_any, first_any, second_any, owner_any,
               kept_ref, place_ref,
               rows_ref, twiddle_ref, common_ref, first_ref, second_ref, owner_ref, parts_ref, sems):
    sources = (rows_any, twiddle_any, common_any, first_any, second_any, owner_any)
    targets = (rows_ref, twiddle_ref, common_ref, first_ref, second_ref, owner_ref)
    copies = [pltpu.make_async_copy(s, t, sems.at[i]) for i, (s, t) in enumerate(zip(sources, targets))]
    for copy in copies:
        copy.start()
    for copy in copies:
        copy.wait()

    owner = owner_ref[...]
    lanes = jnp.broadcast_to(owner, (PAIRS, PAIRS)).astype(jnp.float32)
    earlier = lax.broadcasted_iota(jnp.int32, (PAIRS, PAIRS), 0) < lax.broadcasted_iota(jnp.int32, (PAIRS, PAIRS), 1)
    same = (lanes == lanes.T) & earlier
    slot = jnp.sum(same.astype(jnp.float32), axis=0, keepdims=True).astype(jnp.int32)
    place_ref[...] = one_hot([owner * CAP + slot], place_ref.shape[0]).astype(jnp.bfloat16)
    second = second_ref[...]
    second = second + (second >> 3) * (SLAB - SENSORS)
    kept_ref[RES] = jnp.zeros(kept_ref.shape[1:], jnp.bfloat16)
    kept_ref[RES, pl.ds(0, PICKED), pl.ds(0, TILE)] = one_hot([second + c * SENSORS for c in range(COMPS)], TILE).T.astype(jnp.bfloat16)
    pick_first = one_hot([first_ref[...] + c * SENSORS for c in range(COMPS)], TILE).T.astype(jnp.bfloat16)[:, :SLAB]

    def store(k, value):
        value = padded(value)
        kept_ref[k, pl.ds(PICKED, SLAB), :] = value
        first = jnp.dot(pick_first, value, preferred_element_type=jnp.float32)
        kept_ref[k, pl.ds(0, PICKED), :] = first.astype(jnp.bfloat16)

    forward(rows_ref[...], twiddle_ref, common_ref, parts_ref, store)


def farther_kernel(rows_ref, twiddle_ref, common_ref, white_ref, parts_ref):
    def store(k, value):
        white_ref[k] = padded(value)

    forward(rows_ref[...], twiddle_ref, common_ref, parts_ref, store)


def shares(distances, hour, kept_ref, second_rows_ref, cosines_ref, sines_ref, flip_ref, out_refs, cross_ref, tile_ref):
    count = cross_ref.shape[0]
    base = ((hour ^ distances[0]) >> 2) * (count - 1)
    comps = [base + i for i in range(count)]
    firsts = [lax.div(i, COMPS) for i in comps]
    seconds = [i - f * COMPS for i, f in zip(comps, firsts)]
    group = 16

    def cross(k, carry):
        at_re = pl.ds(pl.multiple_of(k * BINS, BINS), BINS)
        at_im = pl.ds(pl.multiple_of(NB + k * BINS, BINS), BINS)
        for i in range(count):
            for g in range(0, PAIRS, group):
                first_at = pl.ds(pl.multiple_of(firsts[i] * PAIRS + g, group), group)
                second_at = pl.ds(pl.multiple_of(seconds[i] * PAIRS + g, group), group)
                first = kept_ref[k, first_at, :].astype(jnp.float32)
                second = second_rows_ref[k, second_at, :].astype(jnp.float32)
                ar, ai = first[:, :BINS], first[:, BINS:]
                br, bi = second[:, :BINS], second[:, BINS:]
                cross_ref[i, pl.ds(g, group), at_re] = (ar * br + ai * bi).astype(jnp.bfloat16)
                cross_ref[i, pl.ds(g, group), at_im] = (ar * bi - ai * br).astype(jnp.bfloat16)
        return carry

    lax.fori_loop(0, RES, cross, 0)
    block = cross_ref[...].reshape(count * PAIRS, 2 * NB)
    even = jnp.dot(block[:, :NB], cosines_ref[...], preferred_element_type=jnp.float32)
    odd = jnp.dot(block[:, NB:], sines_ref[...], preferred_element_type=jnp.float32)
    zero = jnp.sum(block[:, :NB].astype(jnp.float32), axis=1, keepdims=True)
    later = pltpu.roll(even - odd, 1, axis=1)
    start = lax.broadcasted_iota(jnp.int32, later.shape, 1) == 0
    after = jnp.where(start, zero, later).astype(jnp.bfloat16)
    before = (even + odd).astype(jnp.bfloat16)
    per_comp, per_half = LAGS // TILE, HALF // TILE
    for tile in range(per_half):
        at = tile * TILE
        turned = jnp.dot(before[:, at : at + TILE], flip_ref[...], preferred_element_type=jnp.float32)
        turned = turned.astype(jnp.bfloat16)
        for c in range(count):
            of = slice(c * PAIRS, (c + 1) * PAIRS)
            tile_ref[c * per_comp + per_half - 1 - tile] = turned[of]
            tile_ref[c * per_comp + per_half + tile] = after[of, at : at + TILE]
    for distance, out_ref in zip(distances, out_refs):
        tiles = out_ref.shape[1] // TILE
        begin = (hour ^ distance) * tiles - base * per_comp
        for u in range(tiles):
            out_ref[:, u * TILE : (u + 1) * TILE] = tile_ref[begin + u]


def across_kernel(distances, where_ref, kept_ref, far_ref, sibling_ref, passed_ref, twiddle_ref, common_ref,
                  cosines_ref, sines_ref, flip_ref, *refs):
    *out_refs, second_rows_ref, cross_ref, tile_ref, parts_ref, near_ref, rows_ref = refs

    @pl.when(where_ref[1] == 0)
    def _():
        rows_ref[...] = sibling_ref[...]

    @pl.when(where_ref[1] != 0)
    def _():
        rows_ref[...] = passed_ref[...]

    def store(k, value):
        near_ref[k] = padded(value)

    forward(rows_ref[...], twiddle_ref, common_ref, parts_ref, store)
    pick = kept_ref[RES, pl.ds(0, PICKED), pl.ds(0, TILE)][:, : 3 * SLAB]
    for k in range(RES):
        spectra = jnp.concatenate([kept_ref[k, pl.ds(PICKED, SLAB), :], near_ref[k], far_ref[k]], axis=0)
        second = jnp.dot(pick, spectra, preferred_element_type=jnp.float32)
        second_rows_ref[k] = second.astype(jnp.bfloat16)
    shares(distances, where_ref[0], kept_ref, second_rows_ref, cosines_ref, sines_ref, flip_ref, out_refs, cross_ref,
           tile_ref)


def along_kernel(distances, where_ref, kept_ref, second_rows_ref, cosines_ref, sines_ref, flip_ref, *refs):
    *out_refs, cross_ref, tile_ref = refs
    shares(distances, where_ref[0], kept_ref, second_rows_ref, cosines_ref, sines_ref, flip_ref, out_refs, cross_ref,
           tile_ref)


def total_of(parts_refs):
    total = parts_refs[0][...].astype(jnp.float32)
    for ref in parts_refs[1:]:
        total = total + ref[...].astype(jnp.float32)
    return total


def fold_kernel(*refs):
    *parts_refs, out_ref = refs
    out_ref[...] = total_of(parts_refs).astype(jnp.bfloat16)


def collect_kernel(place_ref, *refs):
    *parts_refs, out_ref = refs
    total = (total_of(parts_refs) * (1.0 / 128.0)).astype(jnp.bfloat16)
    out_ref[...] = jnp.dot(place_ref[...], total, preferred_element_type=jnp.float32).astype(jnp.bfloat16)


def shards(windows, pair_first, pair_second, owners):
    twiddle, common, cosines, sines, flip = (jnp.asarray(t) for t in tables())
    hours = lax.axis_size("hour")
    share = COMPS * COMPS * LAGS // hours
    slots = lax.axis_size("sens") * CAP
    bf16, f32, i32 = jnp.bfloat16, jnp.float32, jnp.int32
    rows = windows[0].transpose(1, 0, 2).reshape(ROWS, SAMPLES)
    sens = lax.axis_size("sens")
    swap = [(s, s ^ 1) for s in range(sens)]
    farther = lax.ppermute(rows, "sens", [(s, (s - 2) % sens) for s in range(sens)])
    sibling = lax.ppermute(rows, "sens", swap)
    where = jnp.stack([lax.axis_index("hour"), lax.axis_index("sens") & 1]).astype(jnp.int32)

    vmem = pl.BlockSpec(memory_space=pltpu.VMEM)
    smem = pl.BlockSpec(memory_space=pltpu.SMEM)
    hbm = pl.BlockSpec(memory_space=pltpu.HBM)
    parts_scratch = pltpu.VMEM((RES * ROWS, 2 * SPAN), f32)
    params = pltpu.CompilerParams(vmem_limit_bytes=16 * MIB)

    spectra = jax.ShapeDtypeStruct((RES, SLAB, 2 * BINS), bf16)

    def cost(flops):
        return pl.CostEstimate(flops=flops, bytes_accessed=10**6, transcendentals=0)

    kept, place = pl.pallas_call(
        own_kernel,
        out_shape=(
            pltpu.VMEM((RES + 1, PICKED + SLAB, 2 * BINS), bf16),
            pltpu.VMEM((slots, PAIRS), bf16),
        ),
        in_specs=[hbm] * 6,
        out_specs=(vmem,) * 2,
        scratch_shapes=[
            pltpu.VMEM((ROWS, SAMPLES), bf16),
            pltpu.VMEM(twiddle.shape, f32),
            pltpu.VMEM(common.shape, bf16),
            pltpu.VMEM((1, PAIRS), i32),
            pltpu.VMEM((1, PAIRS), i32),
            pltpu.VMEM((1, PAIRS), i32),
            parts_scratch,
            pltpu.SemaphoreType.DMA((6,)),
        ],
        compiler_params=pltpu.CompilerParams(vmem_limit_bytes=56 * MIB),
        cost_estimate=cost(10**9),
        name="own",
    )(rows, twiddle, common, *(v.reshape(1, PAIRS) for v in (pair_first, pair_second, owners)))
    farther, place = lax.optimization_barrier((farther, place))
    passed = lax.ppermute(farther, "sens", swap)
    far = pl.pallas_call(
        farther_kernel,
        out_shape=spectra,
        in_specs=[vmem] * 3,
        out_specs=vmem,
        scratch_shapes=[parts_scratch],
        compiler_params=params,
        cost_estimate=cost(10**9),
        name="farther",
    )(farther, twiddle, common)
    one = jax.ShapeDtypeStruct((PAIRS, share), bf16)
    half = COMPS * COMPS // 2 + 1
    shares_scratch = [pltpu.VMEM((half, PAIRS, 2 * NB), bf16), pltpu.VMEM((half * LAGS // TILE, PAIRS, TILE), bf16)]
    big = pltpu.CompilerParams(vmem_limit_bytes=24 * MIB)
    other, same = (7, 6, 5, 4), (3, 2, 1, 0)
    *across, second_rows = pl.pallas_call(
        functools.partial(across_kernel, other),
        out_shape=(one,) * 4 + (jax.ShapeDtypeStruct((RES, PICKED, 2 * BINS), bf16),),
        in_specs=[smem] + [vmem] * 9,
        out_specs=(vmem,) * 5,
        scratch_shapes=shares_scratch + [parts_scratch, pltpu.VMEM((RES, SLAB, 2 * BINS), bf16), pltpu.VMEM((ROWS, SAMPLES), bf16)],
        compiler_params=big,
        cost_estimate=cost(3 * 10**9),
        name="across",
    )(where, kept, far, sibling, passed, twiddle, common, cosines, sines, flip)
    along = pl.pallas_call(
        functools.partial(along_kernel, same),
        out_shape=(one,) * 4,
        in_specs=[smem] + [vmem] * 5,
        out_specs=(vmem,) * 4,
        scratch_shapes=shares_scratch,
        compiler_params=big,
        cost_estimate=cost(3 * 10**9),
        name="along",
    )(where, kept, second_rows, cosines, sines, flip)
    def exchanged(part, distance):
        return lax.ppermute(part, "hour", [(h, h ^ distance) for h in range(hours)]) if distance else part

    folded = pl.pallas_call(
        fold_kernel,
        out_shape=one,
        in_specs=[vmem] * 4,
        out_specs=vmem,
        compiler_params=params,
        cost_estimate=cost(10**7),
        name="fold",
    )(*(exchanged(part, distance & 3) for distance, part in zip(other, across)))
    parts = [exchanged(folded, 4)] + [exchanged(part, distance) for distance, part in zip(same, along)]
    outgoing = pl.pallas_call(
        collect_kernel,
        out_shape=jax.ShapeDtypeStruct((slots, share), bf16),
        in_specs=[vmem] * (1 + len(parts)),
        out_specs=vmem,
        compiler_params=params,
        cost_estimate=cost(2 * 10**7),
        name="collect",
    )(place, *parts)
    stacked = lax.all_to_all(outgoing, "sens", split_axis=0, concat_axis=0, tiled=True)
    return stacked.astype(jnp.float32)


def solution(mesh):
    placed = (P("hour", "sens", None, None), P("sens"), P("sens"), P("sens", None))
    return jax.shard_map(
        shards, mesh=mesh, in_specs=placed, out_specs=P("sens", "hour"), check_vma=False
    )
```

```python
import functools

import jax
import jax.numpy as jnp
import ml_dtypes
import numpy as np
from jax import lax
from jax.experimental import pallas as pl
from jax.experimental.pallas import tpu as pltpu
from jax.sharding import PartitionSpec as P

SAMPLES = 4096
PADDED = 8192
NB = 2048
LAGS = 1024
COMPS = 3
SENSORS = 8
PAIRS = 64
CAP = 4
CHUNKS = 8
SPAN = SAMPLES // CHUNKS
RES = 2 * CHUNKS
BINS = NB // RES
ROWS = COMPS * SENSORS
SLAB = 32
HALF = LAGS // 2
PICKED = COMPS * PAIRS
TILE = 128
MIB = 1 << 20


def tables():
    k = np.arange(1, RES + 1)
    t2 = np.arange(SPAN)
    q = np.arange(BINS)
    angle = 2 * np.pi * ((k[:, None] * t2[None, :]) % PADDED) / PADDED
    twiddle = np.stack([np.cos(angle), -np.sin(angle)]).astype(np.float32)
    period = PADDED // RES
    angle = 2 * np.pi * ((t2[:, None] * q[None, :]) % period) / period
    cos, sin = np.cos(angle), np.sin(angle)
    exact = np.block([[cos, -sin], [sin, cos]])
    high = exact.astype(ml_dtypes.bfloat16)
    common = np.stack([high, (exact - high.astype(np.float64)).astype(ml_dtypes.bfloat16)])
    bins = (k[:, None] + RES * q[None, :]).reshape(-1)
    angle = 2 * np.pi * ((bins[:, None] * np.arange(1, HALF + 1)[None, :]) % PADDED) / PADDED
    cosines = np.cos(angle).astype(ml_dtypes.bfloat16)
    sines = np.sin(angle).astype(ml_dtypes.bfloat16)
    flip = np.eye(TILE)[::-1].astype(ml_dtypes.bfloat16)
    return twiddle, common, cosines, sines, flip


def forward(load, twiddle_ref, common_ref, parts_ref, store):
    chunks = [load(slice(SPAN * i, SPAN * (i + 1))).astype(jnp.float32) for i in range(CHUNKS)]

    def combine(weights, first):
        total = None
        for weight, chunk in zip(weights[first::2], chunks[first::2]):
            weight = float(weight)
            if abs(weight) < 1e-9:
                continue
            term = chunk if abs(weight - 1) < 1e-9 else -chunk if abs(weight + 1) < 1e-9 else chunk * weight
            total = term if total is None else total + term
        return total

    def plus(x, y):
        return y if x is None else x if y is None else x + y

    def minus(x, y):
        return x if y is None else -y if x is None else x - y

    def emit(residue, real_part, imag_part):
        tr = twiddle_ref[0, residue - 1 : residue, :]
        ti = twiddle_ref[1, residue - 1 : residue, :]
        at = pl.ds((residue - 1) * ROWS, ROWS)
        if imag_part is None:
            parts_ref[at, :SPAN] = real_part * tr
            parts_ref[at, SPAN:] = real_part * ti
        else:
            parts_ref[at, :SPAN] = real_part * tr - imag_part * ti
            parts_ref[at, SPAN:] = real_part * ti + imag_part * tr

    half = CHUNKS // 2
    for k in range(half + 1):
        angle = 2 * np.pi * ((k * np.arange(CHUNKS)) % RES) / RES
        re_even, re_odd = combine(np.cos(angle), 0), combine(np.cos(angle), 1)
        im_even, im_odd = combine(-np.sin(angle), 0), combine(-np.sin(angle), 1)
        sums = {k: (plus(re_even, re_odd), plus(im_even, im_odd))}
        if k != half:
            sums[CHUNKS - k] = (minus(re_even, re_odd), minus(im_odd, im_even))
        for residue, (real_part, imag_part) in sums.items():
            emit(residue or RES, real_part, imag_part)
            if residue % CHUNKS:
                emit(RES - residue, real_part, -imag_part)
    both = parts_ref[...]
    high = both.astype(jnp.bfloat16)
    low = (both - high.astype(jnp.float32)).astype(jnp.bfloat16)
    spec = jnp.dot(high, common_ref[0], preferred_element_type=jnp.float32)
    spec = spec + jnp.dot(low, common_ref[0], preferred_element_type=jnp.float32)
    spec = spec + jnp.dot(high, common_ref[1], preferred_element_type=jnp.float32)
    real_part, imag_part = spec[:, :BINS], spec[:, BINS:]
    power = real_part * real_part + imag_part * imag_part
    total = power[:ROWS]
    for k in range(1, RES):
        total = total + power[k * ROWS : (k + 1) * ROWS]
    level = jnp.sum(total, axis=1, keepdims=True) * (1.0 / NB)
    floor = 0.1 * level + 1e-06
    for k in range(RES):
        at = slice(k * ROWS, (k + 1) * ROWS)
        scale = lax.rsqrt(power[at] + floor)
        store(k, jnp.concatenate([real_part[at] * scale, imag_part[at] * scale], axis=1))


def padded(value):
    return jnp.concatenate([value, jnp.zeros((SLAB - ROWS, value.shape[1]), value.dtype)], axis=0).astype(jnp.bfloat16)


def one_hot(index, height):
    at = lax.broadcasted_iota(jnp.int32, (height, PAIRS), 0)
    return jnp.concatenate([(at == i).astype(jnp.float32) for i in index], axis=1)


def own_kernel(rows_any, twiddle_any, common_any, first_any, second_any, owner_any,
               kept_ref, place_ref,
               rows_ref, twiddle_ref, common_ref, first_ref, second_ref, owner_ref, parts_ref, sems):
    sources = (rows_any, twiddle_any, common_any, first_any, second_any, owner_any)
    targets = (rows_ref, twiddle_ref, common_ref, first_ref, second_ref, owner_ref)
    copies = [pltpu.make_async_copy(s, t, sems.at[i]) for i, (s, t) in enumerate(zip(sources, targets))]
    for copy in copies:
        copy.start()
    for copy in copies:
        copy.wait()

    owner = owner_ref[...]
    lanes = jnp.broadcast_to(owner, (PAIRS, PAIRS)).astype(jnp.float32)
    earlier = lax.broadcasted_iota(jnp.int32, (PAIRS, PAIRS), 0) < lax.broadcasted_iota(jnp.int32, (PAIRS, PAIRS), 1)
    same = (lanes == lanes.T) & earlier
    slot = jnp.sum(same.astype(jnp.float32), axis=0, keepdims=True).astype(jnp.int32)
    place_ref[...] = one_hot([owner * CAP + slot], place_ref.shape[0]).astype(jnp.bfloat16)
    second = second_ref[...]
    second = second + (second >> 3) * (SLAB - SENSORS)
    kept_ref[RES] = jnp.zeros(kept_ref.shape[1:], jnp.bfloat16)
    kept_ref[RES, pl.ds(0, PICKED), pl.ds(0, TILE)] = one_hot([second + c * SENSORS for c in range(COMPS)], TILE).T.astype(jnp.bfloat16)
    pick_first = one_hot([first_ref[...] + c * SENSORS for c in range(COMPS)], TILE).T.astype(jnp.bfloat16)[:, :SLAB]

    def store(k, value):
        value = padded(value)
        kept_ref[k, pl.ds(PICKED, SLAB), :] = value
        first = jnp.dot(pick_first, value, preferred_element_type=jnp.float32)
        kept_ref[k, pl.ds(0, PICKED), :] = first.astype(jnp.bfloat16)

    forward(lambda columns: rows_ref[:, columns], twiddle_ref, common_ref, parts_ref, store)


def farther_kernel(rows_ref, twiddle_ref, common_ref, white_ref, parts_ref):
    def store(k, value):
        white_ref[k] = padded(value)

    forward(lambda columns: rows_ref[:, columns], twiddle_ref, common_ref, parts_ref, store)


def nearer_kernel(where_ref, sibling_ref, passed_ref, twiddle_ref, common_ref, white_ref, parts_ref):
    odd = where_ref[1] != 0

    def store(k, value):
        white_ref[k] = padded(value)

    def load(columns):
        return jnp.where(odd, passed_ref[:, columns].astype(jnp.float32), sibling_ref[:, columns].astype(jnp.float32))

    forward(load, twiddle_ref, common_ref, parts_ref, store)


def shares(distances, hour, kept_ref, second_rows_ref, cosines_ref, sines_ref, flip_ref, out_refs, cross_ref, tile_ref,
           prepare=lambda k: None):
    count = cross_ref.shape[0]
    base = ((hour ^ distances[0]) >> 2) * (count - 1)
    comps = [base + i for i in range(count)]
    firsts = [lax.div(i, COMPS) for i in comps]
    seconds = [i - f * COMPS for i, f in zip(comps, firsts)]
    group = 16

    def cross(k):
        for i in range(count):
            for g in range(0, PAIRS, group):
                first_at = pl.ds(pl.multiple_of(firsts[i] * PAIRS + g, group), group)
                second_at = pl.ds(pl.multiple_of(seconds[i] * PAIRS + g, group), group)
                first = kept_ref[k, first_at, :].astype(jnp.float32)
                second = second_rows_ref[k, second_at, :].astype(jnp.float32)
                ar, ai = first[:, :BINS], first[:, BINS:]
                br, bi = second[:, :BINS], second[:, BINS:]
                at = pl.ds(g, group)
                cross_ref[i, at, pl.ds(k * BINS, BINS)] = (ar * br + ai * bi).astype(jnp.bfloat16)
                cross_ref[i, at, pl.ds(NB + k * BINS, BINS)] = (ar * bi - ai * br).astype(jnp.bfloat16)

    def rows(start, width):
        return cross_ref[:, :, pl.ds(start, width)].reshape(count * PAIRS, width)

    def plus(x, y):
        return y if x is None else x + y

    steps = 4
    each = RES // steps
    width = NB // steps
    even = odd = zero = None
    for step in range(steps + 1):
        for k in range(each * 2) if step == 0 else range((step + 1) * each, min((step + 2) * each, RES)):
            prepare(k)
        for k in range(step * each, min((step + 1) * each, RES)):
            cross(k)
        if step:
            at = (step - 1) * width
            real_part, imag_part = rows(at, width), rows(NB + at, width)
            even = plus(even, jnp.dot(real_part, cosines_ref[pl.ds(at, width), :], preferred_element_type=jnp.float32))
            odd = plus(odd, jnp.dot(imag_part, sines_ref[pl.ds(at, width), :], preferred_element_type=jnp.float32))
            zero = plus(zero, jnp.sum(real_part.astype(jnp.float32), axis=1, keepdims=True))
    later = pltpu.roll(even - odd, 1, axis=1)
    start = lax.broadcasted_iota(jnp.int32, later.shape, 1) == 0
    after = jnp.where(start, zero, later).astype(jnp.bfloat16)
    before = (even + odd).astype(jnp.bfloat16)
    per_comp, per_half = LAGS // TILE, HALF // TILE
    for tile in range(per_half):
        at = tile * TILE
        turned = jnp.dot(before[:, at : at + TILE], flip_ref[...], preferred_element_type=jnp.float32)
        turned = turned.astype(jnp.bfloat16)
        for c in range(count):
            of = slice(c * PAIRS, (c + 1) * PAIRS)
            tile_ref[c * per_comp + per_half - 1 - tile] = turned[of]
            tile_ref[c * per_comp + per_half + tile] = after[of, at : at + TILE]
    for distance, out_ref in zip(distances, out_refs):
        tiles = out_ref.shape[1] // TILE
        begin = (hour ^ distance) * tiles - base * per_comp
        for u in range(tiles):
            out_ref[:, u * TILE : (u + 1) * TILE] = tile_ref[begin + u]


def across_kernel(distances, where_ref, kept_ref, near_ref, far_ref, cosines_ref, sines_ref, flip_ref, *refs):
    *out_refs, second_rows_ref, cross_ref, tile_ref = refs
    pick = kept_ref[RES, pl.ds(0, PICKED), pl.ds(0, TILE)][:, : 3 * SLAB]

    def prepare(k):
        spectra = jnp.concatenate([kept_ref[k, pl.ds(PICKED, SLAB), :], near_ref[k], far_ref[k]], axis=0)
        second = jnp.dot(pick, spectra, preferred_element_type=jnp.float32)
        second_rows_ref[k] = second.astype(jnp.bfloat16)

    shares(distances, where_ref[0], kept_ref, second_rows_ref, cosines_ref, sines_ref, flip_ref, out_refs, cross_ref,
           tile_ref, prepare)


def along_kernel(distances, where_ref, kept_ref, second_rows_ref, cosines_ref, sines_ref, flip_ref, *refs):
    *out_refs, cross_ref, tile_ref = refs
    shares(distances, where_ref[0], kept_ref, second_rows_ref, cosines_ref, sines_ref, flip_ref, out_refs, cross_ref,
           tile_ref)


def total_of(parts_refs):
    total = parts_refs[0][...].astype(jnp.float32)
    for ref in parts_refs[1:]:
        total = total + ref[...].astype(jnp.float32)
    return total


def fold_kernel(*refs):
    *parts_refs, out_ref = refs
    out_ref[...] = total_of(parts_refs).astype(jnp.bfloat16)


def collect_kernel(place_ref, *refs):
    *parts_refs, out_ref = refs
    total = (total_of(parts_refs) * (1.0 / 128.0)).astype(jnp.bfloat16)
    out_ref[...] = jnp.dot(place_ref[...], total, preferred_element_type=jnp.float32).astype(jnp.bfloat16)


def shards(windows, pair_first, pair_second, owners):
    twiddle, common, cosines, sines, flip = (jnp.asarray(t) for t in tables())
    hours = lax.axis_size("hour")
    share = COMPS * COMPS * LAGS // hours
    slots = lax.axis_size("sens") * CAP
    bf16, f32, i32 = jnp.bfloat16, jnp.float32, jnp.int32
    rows = windows[0].transpose(1, 0, 2).reshape(ROWS, SAMPLES)
    sens = lax.axis_size("sens")
    swap = [(s, s ^ 1) for s in range(sens)]
    farther = lax.ppermute(rows, "sens", [(s, (s - 2) % sens) for s in range(sens)])
    sibling = lax.ppermute(rows, "sens", swap)
    where = jnp.stack([lax.axis_index("hour"), lax.axis_index("sens") & 1]).astype(jnp.int32)

    vmem = pl.BlockSpec(memory_space=pltpu.VMEM)
    smem = pl.BlockSpec(memory_space=pltpu.SMEM)
    hbm = pl.BlockSpec(memory_space=pltpu.HBM)
    parts_scratch = pltpu.VMEM((RES * ROWS, 2 * SPAN), f32)
    params = pltpu.CompilerParams(vmem_limit_bytes=16 * MIB)

    spectra = jax.ShapeDtypeStruct((RES, SLAB, 2 * BINS), bf16)

    def cost(flops):
        return pl.CostEstimate(flops=flops, bytes_accessed=10**6, transcendentals=0)

    kept, place = pl.pallas_call(
        own_kernel,
        out_shape=(
            pltpu.VMEM((RES + 1, PICKED + SLAB, 2 * BINS), bf16),
            pltpu.VMEM((slots, PAIRS), bf16),
        ),
        in_specs=[hbm] * 6,
        out_specs=(vmem,) * 2,
        scratch_shapes=[
            pltpu.VMEM((ROWS, SAMPLES), bf16),
            pltpu.VMEM(twiddle.shape, f32),
            pltpu.VMEM(common.shape, bf16),
            pltpu.VMEM((1, PAIRS), i32),
            pltpu.VMEM((1, PAIRS), i32),
            pltpu.VMEM((1, PAIRS), i32),
            parts_scratch,
            pltpu.SemaphoreType.DMA((6,)),
        ],
        compiler_params=pltpu.CompilerParams(vmem_limit_bytes=56 * MIB),
        cost_estimate=cost(10**9),
        name="own",
    )(rows, twiddle, common, *(v.reshape(1, PAIRS) for v in (pair_first, pair_second, owners)))
    farther, place = lax.optimization_barrier((farther, place))
    passed = lax.ppermute(farther, "sens", swap)

    def whitened(kernel, name, in_specs, args):
        return pl.pallas_call(
            kernel,
            out_shape=spectra,
            in_specs=in_specs,
            out_specs=vmem,
            scratch_shapes=[parts_scratch],
            compiler_params=params,
            cost_estimate=cost(10**9),
            name=name,
        )(*args, twiddle, common)

    far = whitened(farther_kernel, "farther", [vmem] * 3, (farther,))
    near = whitened(nearer_kernel, "nearer", [smem] + [vmem] * 4, (where, sibling, passed))
    one = jax.ShapeDtypeStruct((PAIRS, share), bf16)
    half = COMPS * COMPS // 2 + 1
    shares_scratch = [pltpu.VMEM((half, PAIRS, 2 * NB), bf16), pltpu.VMEM((half * LAGS // TILE, PAIRS, TILE), bf16)]
    big = pltpu.CompilerParams(vmem_limit_bytes=24 * MIB)
    other, same = (7, 6, 5, 4), (3, 2, 1, 0)
    *across, second_rows = pl.pallas_call(
        functools.partial(across_kernel, other),
        out_shape=(one,) * 4 + (jax.ShapeDtypeStruct((RES, PICKED, 2 * BINS), bf16),),
        in_specs=[smem] + [vmem] * 6,
        out_specs=(vmem,) * 5,
        scratch_shapes=shares_scratch,
        compiler_params=big,
        cost_estimate=cost(3 * 10**9),
        name="across",
    )(where, kept, near, far, cosines, sines, flip)
    along = pl.pallas_call(
        functools.partial(along_kernel, same),
        out_shape=(one,) * 4,
        in_specs=[smem] + [vmem] * 5,
        out_specs=(vmem,) * 4,
        scratch_shapes=shares_scratch,
        compiler_params=big,
        cost_estimate=cost(3 * 10**9),
        name="along",
    )(where, kept, second_rows, cosines, sines, flip)
    def exchanged(part, distance):
        return lax.ppermute(part, "hour", [(h, h ^ distance) for h in range(hours)]) if distance else part

    folded = pl.pallas_call(
        fold_kernel,
        out_shape=one,
        in_specs=[vmem] * 4,
        out_specs=vmem,
        compiler_params=params,
        cost_estimate=cost(10**7),
        name="fold",
    )(*(exchanged(part, distance & 3) for distance, part in zip(other, across)))
    parts = [exchanged(folded, 4)] + [exchanged(part, distance) for distance, part in zip(same, along)]
    outgoing = pl.pallas_call(
        collect_kernel,
        out_shape=jax.ShapeDtypeStruct((slots, share), bf16),
        in_specs=[vmem] * (1 + len(parts)),
        out_specs=vmem,
        compiler_params=params,
        cost_estimate=cost(2 * 10**7),
        name="collect",
    )(place, *parts)
    stacked = lax.all_to_all(outgoing, "sens", split_axis=0, concat_axis=0, tiled=True)
    return stacked.astype(jnp.float32)


def solution(mesh):
    placed = (P("hour", "sens", None, None), P("sens"), P("sens"), P("sens", None))
    return jax.shard_map(
        shards, mesh=mesh, in_specs=placed, out_specs=P("sens", "hour"), check_vma=False
    )
```

```python
import functools

import jax
import jax.numpy as jnp
import ml_dtypes
import numpy as np
from jax import lax
from jax.experimental import pallas as pl
from jax.experimental.pallas import tpu as pltpu
from jax.sharding import PartitionSpec as P

SAMPLES = 4096
PADDED = 8192
NB = 2048
LAGS = 1024
COMPS = 3
SENSORS = 8
PAIRS = 64
CAP = 4
CHUNKS = 8
SPAN = SAMPLES // CHUNKS
RES = 2 * CHUNKS
BINS = NB // RES
ROWS = COMPS * SENSORS
SLAB = 32
HALF = LAGS // 2
PICKED = COMPS * PAIRS
TILE = 128
MIB = 1 << 20


def tables():
    k = np.arange(1, RES + 1)
    t2 = np.arange(SPAN)
    q = np.arange(BINS)
    angle = 2 * np.pi * ((k[:, None] * t2[None, :]) % PADDED) / PADDED
    twiddle = np.stack([np.cos(angle), -np.sin(angle)]).astype(np.float32)
    period = PADDED // RES
    angle = 2 * np.pi * ((t2[:, None] * q[None, :]) % period) / period
    cos, sin = np.cos(angle), np.sin(angle)
    exact = np.block([[cos, -sin], [sin, cos]])
    high = exact.astype(ml_dtypes.bfloat16)
    common = np.stack([high, (exact - high.astype(np.float64)).astype(ml_dtypes.bfloat16)])
    bins = (k[:, None] + RES * q[None, :]).reshape(-1)
    angle = 2 * np.pi * ((bins[:, None] * np.arange(1, HALF + 1)[None, :]) % PADDED) / PADDED
    cosines = np.cos(angle).astype(ml_dtypes.bfloat16)
    sines = np.sin(angle).astype(ml_dtypes.bfloat16)
    flip = np.eye(TILE)[::-1].astype(ml_dtypes.bfloat16)
    return twiddle, common, cosines, sines, flip


def forward(load, twiddle_ref, common_ref, parts_ref, store):
    chunks = [load(slice(SPAN * i, SPAN * (i + 1))).astype(jnp.float32) for i in range(CHUNKS)]

    def combine(weights, first):
        total = None
        for weight, chunk in zip(weights[first::2], chunks[first::2]):
            weight = float(weight)
            if abs(weight) < 1e-9:
                continue
            term = chunk if abs(weight - 1) < 1e-9 else -chunk if abs(weight + 1) < 1e-9 else chunk * weight
            total = term if total is None else total + term
        return total

    def plus(x, y):
        return y if x is None else x if y is None else x + y

    def minus(x, y):
        return x if y is None else -y if x is None else x - y

    def emit(residue, real_part, imag_part):
        tr = twiddle_ref[0, residue - 1 : residue, :]
        ti = twiddle_ref[1, residue - 1 : residue, :]
        at = pl.ds((residue - 1) * ROWS, ROWS)
        if imag_part is None:
            parts_ref[at, :SPAN] = real_part * tr
            parts_ref[at, SPAN:] = real_part * ti
        else:
            parts_ref[at, :SPAN] = real_part * tr - imag_part * ti
            parts_ref[at, SPAN:] = real_part * ti + imag_part * tr

    half = CHUNKS // 2
    for k in range(half + 1):
        angle = 2 * np.pi * ((k * np.arange(CHUNKS)) % RES) / RES
        re_even, re_odd = combine(np.cos(angle), 0), combine(np.cos(angle), 1)
        im_even, im_odd = combine(-np.sin(angle), 0), combine(-np.sin(angle), 1)
        sums = {k: (plus(re_even, re_odd), plus(im_even, im_odd))}
        if k != half:
            sums[CHUNKS - k] = (minus(re_even, re_odd), minus(im_odd, im_even))
        for residue, (real_part, imag_part) in sums.items():
            emit(residue or RES, real_part, imag_part)
            if residue % CHUNKS:
                emit(RES - residue, real_part, -imag_part)
    both = parts_ref[...]
    high = both.astype(jnp.bfloat16)
    low = (both - high.astype(jnp.float32)).astype(jnp.bfloat16)
    spec = jnp.dot(high, common_ref[0], preferred_element_type=jnp.float32)
    spec = spec + jnp.dot(low, common_ref[0], preferred_element_type=jnp.float32)
    spec = spec + jnp.dot(high, common_ref[1], preferred_element_type=jnp.float32)
    real_part, imag_part = spec[:, :BINS], spec[:, BINS:]
    power = real_part * real_part + imag_part * imag_part
    total = power[:ROWS]
    for k in range(1, RES):
        total = total + power[k * ROWS : (k + 1) * ROWS]
    level = jnp.sum(total, axis=1, keepdims=True) * (1.0 / NB)
    floor = 0.1 * level + 1e-06
    for k in range(RES):
        at = slice(k * ROWS, (k + 1) * ROWS)
        scale = lax.rsqrt(power[at] + floor)
        store(k, jnp.concatenate([real_part[at] * scale, imag_part[at] * scale], axis=1))


def padded(value):
    return jnp.concatenate([value, jnp.zeros((SLAB - ROWS, value.shape[1]), value.dtype)], axis=0).astype(jnp.bfloat16)


def one_hot(index, height):
    at = lax.broadcasted_iota(jnp.int32, (height, PAIRS), 0)
    return jnp.concatenate([(at == i).astype(jnp.float32) for i in index], axis=1)


def own_kernel(rows_any, twiddle_any, common_any, first_any, second_any, owner_any,
               kept_ref, place_ref,
               rows_ref, twiddle_ref, common_ref, first_ref, second_ref, owner_ref, parts_ref, sems):
    sources = (rows_any, twiddle_any, common_any, first_any, second_any, owner_any)
    targets = (rows_ref, twiddle_ref, common_ref, first_ref, second_ref, owner_ref)
    copies = [pltpu.make_async_copy(s, t, sems.at[i]) for i, (s, t) in enumerate(zip(sources, targets))]
    for copy in copies:
        copy.start()
    for copy in copies:
        copy.wait()

    owner = owner_ref[...]
    lanes = jnp.broadcast_to(owner, (PAIRS, PAIRS)).astype(jnp.float32)
    earlier = lax.broadcasted_iota(jnp.int32, (PAIRS, PAIRS), 0) < lax.broadcasted_iota(jnp.int32, (PAIRS, PAIRS), 1)
    same = (lanes == lanes.T) & earlier
    slot = jnp.sum(same.astype(jnp.float32), axis=0, keepdims=True).astype(jnp.int32)
    place_ref[...] = one_hot([owner * CAP + slot], place_ref.shape[0]).astype(jnp.bfloat16)
    second = second_ref[...]
    second = second + (second >> 3) * (SLAB - SENSORS)
    kept_ref[RES] = jnp.zeros(kept_ref.shape[1:], jnp.bfloat16)
    kept_ref[RES, pl.ds(0, PICKED), pl.ds(0, TILE)] = one_hot([second + c * SENSORS for c in range(COMPS)], TILE).T.astype(jnp.bfloat16)
    pick_first = one_hot([first_ref[...] + c * SENSORS for c in range(COMPS)], TILE).T.astype(jnp.bfloat16)[:, :SLAB]

    def store(k, value):
        value = padded(value)
        kept_ref[k, pl.ds(PICKED, SLAB), :] = value
        first = jnp.dot(pick_first, value, preferred_element_type=jnp.float32)
        kept_ref[k, pl.ds(0, PICKED), :] = first.astype(jnp.bfloat16)

    forward(lambda columns: rows_ref[:, columns], twiddle_ref, common_ref, parts_ref, store)


def farther_kernel(rows_ref, twiddle_ref, common_ref, white_ref, parts_ref):
    def store(k, value):
        white_ref[k] = padded(value)

    forward(lambda columns: rows_ref[:, columns], twiddle_ref, common_ref, parts_ref, store)


def nearer_kernel(sibling_ref, passed_ref, twiddle_ref, common_ref, white_ref, parts_ref):
    odd = lax.axis_index("sens") & 1

    def store(k, value):
        white_ref[k] = padded(value)

    for parity, rows_ref in ((0, sibling_ref), (1, passed_ref)):
        @pl.when(odd == parity)
        def _(rows_ref=rows_ref):
            forward(lambda columns: rows_ref[:, columns], twiddle_ref, common_ref, parts_ref, store)


def shares(distances, hour, kept_ref, second_rows_ref, cosines_ref, sines_ref, flip_ref, out_refs, cross_ref, tile_ref,
           prepare=lambda k: None):
    count = cross_ref.shape[0]
    base = ((hour ^ distances[0]) >> 2) * (count - 1)
    comps = [base + i for i in range(count)]
    firsts = [lax.div(i, COMPS) for i in comps]
    seconds = [i - f * COMPS for i, f in zip(comps, firsts)]
    group = 16

    def cross(k):
        for i in range(count):
            for g in range(0, PAIRS, group):
                first_at = pl.ds(pl.multiple_of(firsts[i] * PAIRS + g, group), group)
                second_at = pl.ds(pl.multiple_of(seconds[i] * PAIRS + g, group), group)
                first = kept_ref[k, first_at, :].astype(jnp.float32)
                second = second_rows_ref[k, second_at, :].astype(jnp.float32)
                ar, ai = first[:, :BINS], first[:, BINS:]
                br, bi = second[:, :BINS], second[:, BINS:]
                at = pl.ds(g, group)
                cross_ref[i, at, pl.ds(k * BINS, BINS)] = (ar * br + ai * bi).astype(jnp.bfloat16)
                cross_ref[i, at, pl.ds(NB + k * BINS, BINS)] = (ar * bi - ai * br).astype(jnp.bfloat16)

    def rows(start, width):
        return cross_ref[:, :, pl.ds(start, width)].reshape(count * PAIRS, width)

    def plus(x, y):
        return y if x is None else x + y

    steps = 4
    each = RES // steps
    width = NB // steps
    even = odd = zero = None
    for step in range(steps + 1):
        for k in range(each * 2) if step == 0 else range((step + 1) * each, min((step + 2) * each, RES)):
            prepare(k)
        for k in range(step * each, min((step + 1) * each, RES)):
            cross(k)
        if step:
            at = (step - 1) * width
            real_part, imag_part = rows(at, width), rows(NB + at, width)
            even = plus(even, jnp.dot(real_part, cosines_ref[pl.ds(at, width), :], preferred_element_type=jnp.float32))
            odd = plus(odd, jnp.dot(imag_part, sines_ref[pl.ds(at, width), :], preferred_element_type=jnp.float32))
            zero = plus(zero, jnp.sum(real_part.astype(jnp.float32), axis=1, keepdims=True))
    later = pltpu.roll(even - odd, 1, axis=1)
    start = lax.broadcasted_iota(jnp.int32, later.shape, 1) == 0
    after = jnp.where(start, zero, later).astype(jnp.bfloat16)
    before = (even + odd).astype(jnp.bfloat16)
    per_comp, per_half = LAGS // TILE, HALF // TILE
    for tile in range(per_half):
        at = tile * TILE
        turned = jnp.dot(before[:, at : at + TILE], flip_ref[...], preferred_element_type=jnp.float32)
        turned = turned.astype(jnp.bfloat16)
        for c in range(count):
            of = slice(c * PAIRS, (c + 1) * PAIRS)
            tile_ref[c * per_comp + per_half - 1 - tile] = turned[of]
            tile_ref[c * per_comp + per_half + tile] = after[of, at : at + TILE]
    for distance, out_ref in zip(distances, out_refs):
        tiles = out_ref.shape[1] // TILE
        begin = (hour ^ distance) * tiles - base * per_comp
        for u in range(tiles):
            out_ref[:, u * TILE : (u + 1) * TILE] = tile_ref[begin + u]


def across_kernel(distances, kept_ref, near_ref, far_ref, cosines_ref, sines_ref, flip_ref, *refs):
    *out_refs, second_rows_ref, cross_ref, tile_ref = refs
    pick = kept_ref[RES, pl.ds(0, PICKED), pl.ds(0, TILE)][:, : 3 * SLAB]

    def prepare(k):
        spectra = jnp.concatenate([kept_ref[k, pl.ds(PICKED, SLAB), :], near_ref[k], far_ref[k]], axis=0)
        second = jnp.dot(pick, spectra, preferred_element_type=jnp.float32)
        second_rows_ref[k] = second.astype(jnp.bfloat16)

    shares(distances, lax.axis_index("hour"), kept_ref, second_rows_ref, cosines_ref, sines_ref, flip_ref, out_refs, cross_ref,
           tile_ref, prepare)


def along_kernel(distances, kept_ref, second_rows_ref, cosines_ref, sines_ref, flip_ref, *refs):
    *out_refs, cross_ref, tile_ref = refs
    shares(distances, lax.axis_index("hour"), kept_ref, second_rows_ref, cosines_ref, sines_ref, flip_ref, out_refs, cross_ref,
           tile_ref)


def total_of(parts_refs):
    total = parts_refs[0][...].astype(jnp.float32)
    for ref in parts_refs[1:]:
        total = total + ref[...].astype(jnp.float32)
    return total


def fold_kernel(*refs):
    *parts_refs, out_ref = refs
    out_ref[...] = total_of(parts_refs).astype(jnp.bfloat16)


def collect_kernel(place_ref, *refs):
    *parts_refs, out_ref = refs
    total = (total_of(parts_refs) * (1.0 / 128.0)).astype(jnp.bfloat16)
    out_ref[...] = jnp.dot(place_ref[...], total, preferred_element_type=jnp.float32).astype(jnp.bfloat16)


def shards(windows, pair_first, pair_second, owners):
    twiddle, common, cosines, sines, flip = (jnp.asarray(t) for t in tables())
    hours = lax.axis_size("hour")
    share = COMPS * COMPS * LAGS // hours
    slots = lax.axis_size("sens") * CAP
    bf16, f32, i32 = jnp.bfloat16, jnp.float32, jnp.int32
    rows = windows[0].transpose(1, 0, 2).reshape(ROWS, SAMPLES)
    sens = lax.axis_size("sens")
    swap = [(s, s ^ 1) for s in range(sens)]
    farther = lax.ppermute(rows, "sens", [(s, (s - 2) % sens) for s in range(sens)])
    sibling = lax.ppermute(rows, "sens", swap)

    vmem = pl.BlockSpec(memory_space=pltpu.VMEM)
    hbm = pl.BlockSpec(memory_space=pltpu.HBM)
    parts_scratch = pltpu.VMEM((RES * ROWS, 2 * SPAN), f32)
    params = pltpu.CompilerParams(vmem_limit_bytes=16 * MIB)

    spectra = jax.ShapeDtypeStruct((RES, SLAB, 2 * BINS), bf16)

    def cost(flops):
        return pl.CostEstimate(flops=flops, bytes_accessed=10**6, transcendentals=0)

    kept, place = pl.pallas_call(
        own_kernel,
        out_shape=(
            pltpu.VMEM((RES + 1, PICKED + SLAB, 2 * BINS), bf16),
            pltpu.VMEM((slots, PAIRS), bf16),
        ),
        in_specs=[hbm] * 6,
        out_specs=(vmem,) * 2,
        scratch_shapes=[
            pltpu.VMEM((ROWS, SAMPLES), bf16),
            pltpu.VMEM(twiddle.shape, f32),
            pltpu.VMEM(common.shape, bf16),
            pltpu.VMEM((1, PAIRS), i32),
            pltpu.VMEM((1, PAIRS), i32),
            pltpu.VMEM((1, PAIRS), i32),
            parts_scratch,
            pltpu.SemaphoreType.DMA((6,)),
        ],
        compiler_params=pltpu.CompilerParams(vmem_limit_bytes=56 * MIB),
        cost_estimate=cost(10000000000),
        name="own",
    )(rows, twiddle, common, *(v.reshape(1, PAIRS) for v in (pair_first, pair_second, owners)))
    farther, place = lax.optimization_barrier((farther, place))
    passed = lax.ppermute(farther, "sens", swap)

    def whitened(kernel, name, in_specs, args):
        return pl.pallas_call(
            kernel,
            out_shape=spectra,
            in_specs=in_specs,
            out_specs=vmem,
            scratch_shapes=[parts_scratch],
            compiler_params=params,
            cost_estimate=cost(700000000),
            name=name,
        )(*args, twiddle, common)

    far = whitened(farther_kernel, "farther", [vmem] * 3, (farther,))
    near = whitened(nearer_kernel, "nearer", [vmem] * 4, (sibling, passed))
    one = jax.ShapeDtypeStruct((PAIRS, share), bf16)
    half = COMPS * COMPS // 2 + 1
    shares_scratch = [pltpu.VMEM((half, PAIRS, 2 * NB), bf16), pltpu.VMEM((half * LAGS // TILE, PAIRS, TILE), bf16)]
    big = pltpu.CompilerParams(vmem_limit_bytes=24 * MIB)
    other, same = (7, 6, 5, 4), (3, 2, 1, 0)
    *across, second_rows = pl.pallas_call(
        functools.partial(across_kernel, other),
        out_shape=(one,) * 4 + (jax.ShapeDtypeStruct((RES, PICKED, 2 * BINS), bf16),),
        in_specs=[vmem] * 6,
        out_specs=(vmem,) * 5,
        scratch_shapes=shares_scratch,
        compiler_params=big,
        cost_estimate=cost(3 * 10**9),
        name="across",
    )(kept, near, far, cosines, sines, flip)
    along = pl.pallas_call(
        functools.partial(along_kernel, same),
        out_shape=(one,) * 4,
        in_specs=[vmem] * 5,
        out_specs=(vmem,) * 4,
        scratch_shapes=shares_scratch,
        compiler_params=big,
        cost_estimate=cost(3 * 10**9),
        name="along",
    )(kept, second_rows, cosines, sines, flip)
    def exchanged(part, distance):
        return lax.ppermute(part, "hour", [(h, h ^ distance) for h in range(hours)]) if distance else part

    def fold(*shares_here):
        return pl.pallas_call(
            fold_kernel,
            out_shape=one,
            in_specs=[vmem] * len(shares_here),
            out_specs=vmem,
            compiler_params=params,
            cost_estimate=cost(10**7),
            name="fold",
        )(*shares_here)

    far_y, far_two, far_one, far_here = across
    same_y, same_two, same_one, same_here = along
    joined = exchanged(far_two, 4)
    folded = fold(exchanged(far_y, 3), exchanged(far_one, 1), far_here)
    parts = [
        exchanged(folded, 4),
        exchanged(same_y, 3),
        exchanged(same_one, 1),
        exchanged(fold(same_two, joined), 2),
        same_here,
    ]
    outgoing = pl.pallas_call(
        collect_kernel,
        out_shape=jax.ShapeDtypeStruct((slots, share), bf16),
        in_specs=[vmem] * (1 + len(parts)),
        out_specs=vmem,
        compiler_params=params,
        cost_estimate=cost(2 * 10**7),
        name="collect",
    )(place, *parts)
    stacked = lax.all_to_all(outgoing, "sens", split_axis=0, concat_axis=0, tiled=True)
    return stacked.astype(jnp.float32)


def solution(mesh):
    placed = (P("hour", "sens", None, None), P("sens"), P("sens"), P("sens", None))
    return jax.shard_map(
        shards, mesh=mesh, in_specs=placed, out_specs=P("sens", "hour"), check_vma=False
    )
```

```python
import functools

import jax
import jax.numpy as jnp
import ml_dtypes
import numpy as np
from jax import lax
from jax.experimental import pallas as pl
from jax.experimental.pallas import tpu as pltpu
from jax.sharding import PartitionSpec as P

SAMPLES = 4096
PADDED = 8192
NB = 2048
LAGS = 1024
COMPS = 3
SENSORS = 8
PAIRS = 64
CAP = 4
CHUNKS = 8
SPAN = SAMPLES // CHUNKS
RES = 2 * CHUNKS
BINS = NB // RES
ROWS = COMPS * SENSORS
SLAB = 32
HALF = LAGS // 2
PICKED = COMPS * PAIRS
TILE = 128
MIB = 1 << 20


def tables():
    k = np.arange(1, RES + 1)
    t2 = np.arange(SPAN)
    q = np.arange(BINS)
    angle = 2 * np.pi * ((k[:, None] * t2[None, :]) % PADDED) / PADDED
    twiddle = np.stack([np.cos(angle), -np.sin(angle)]).astype(np.float32)
    period = PADDED // RES
    angle = 2 * np.pi * ((t2[:, None] * q[None, :]) % period) / period
    cos, sin = np.cos(angle), np.sin(angle)
    exact = np.block([[cos, -sin], [sin, cos]])
    high = exact.astype(ml_dtypes.bfloat16)
    common = np.stack([high, (exact - high.astype(np.float64)).astype(ml_dtypes.bfloat16)])
    bins = (k[:, None] + RES * q[None, :]).reshape(-1)
    angle = 2 * np.pi * ((bins[:, None] * np.arange(1, HALF + 1)[None, :]) % PADDED) / PADDED
    cosines = np.cos(angle).astype(ml_dtypes.bfloat16)
    sines = np.sin(angle).astype(ml_dtypes.bfloat16)
    flip = np.eye(TILE)[::-1].astype(ml_dtypes.bfloat16)
    return twiddle, common, cosines, sines, flip


def forward(load, twiddle_ref, common_ref, parts_ref, store):
    chunks = [load(slice(SPAN * i, SPAN * (i + 1))).astype(jnp.float32) for i in range(CHUNKS)]

    def combine(weights, first):
        total = None
        for weight, chunk in zip(weights[first::2], chunks[first::2]):
            weight = float(weight)
            if abs(weight) < 1e-9:
                continue
            term = chunk if abs(weight - 1) < 1e-9 else -chunk if abs(weight + 1) < 1e-9 else chunk * weight
            total = term if total is None else total + term
        return total

    def plus(x, y):
        return y if x is None else x if y is None else x + y

    def minus(x, y):
        return x if y is None else -y if x is None else x - y

    def emit(residue, real_part, imag_part):
        tr = twiddle_ref[0, residue - 1 : residue, :]
        ti = twiddle_ref[1, residue - 1 : residue, :]
        at = pl.ds((residue - 1) * ROWS, ROWS)
        if imag_part is None:
            parts_ref[at, :SPAN] = real_part * tr
            parts_ref[at, SPAN:] = real_part * ti
        else:
            parts_ref[at, :SPAN] = real_part * tr - imag_part * ti
            parts_ref[at, SPAN:] = real_part * ti + imag_part * tr

    half = CHUNKS // 2
    for k in range(half + 1):
        angle = 2 * np.pi * ((k * np.arange(CHUNKS)) % RES) / RES
        re_even, re_odd = combine(np.cos(angle), 0), combine(np.cos(angle), 1)
        im_even, im_odd = combine(-np.sin(angle), 0), combine(-np.sin(angle), 1)
        sums = {k: (plus(re_even, re_odd), plus(im_even, im_odd))}
        if k != half:
            sums[CHUNKS - k] = (minus(re_even, re_odd), minus(im_odd, im_even))
        for residue, (real_part, imag_part) in sums.items():
            emit(residue or RES, real_part, imag_part)
            if residue % CHUNKS:
                emit(RES - residue, real_part, -imag_part)
    both = parts_ref[...]
    high = both.astype(jnp.bfloat16)
    low = (both - high.astype(jnp.float32)).astype(jnp.bfloat16)
    spec = jnp.dot(high, common_ref[0], preferred_element_type=jnp.float32)
    spec = spec + jnp.dot(low, common_ref[0], preferred_element_type=jnp.float32)
    spec = spec + jnp.dot(high, common_ref[1], preferred_element_type=jnp.float32)
    real_part, imag_part = spec[:, :BINS], spec[:, BINS:]
    power = real_part * real_part + imag_part * imag_part
    total = power[:ROWS]
    for k in range(1, RES):
        total = total + power[k * ROWS : (k + 1) * ROWS]
    level = jnp.sum(total, axis=1, keepdims=True) * (1.0 / NB)
    floor = 0.1 * level + 1e-06
    for k in range(RES):
        at = slice(k * ROWS, (k + 1) * ROWS)
        scale = lax.rsqrt(power[at] + floor)
        store(k, jnp.concatenate([real_part[at] * scale, imag_part[at] * scale], axis=1))


def padded(value):
    return jnp.concatenate([value, jnp.zeros((SLAB - ROWS, value.shape[1]), value.dtype)], axis=0).astype(jnp.bfloat16)


def one_hot(index, height):
    at = lax.broadcasted_iota(jnp.int32, (height, PAIRS), 0)
    return jnp.concatenate([(at == i).astype(jnp.float32) for i in index], axis=1)


def own_kernel(rows_any, twiddle_any, common_any, first_any, second_any, owner_any,
               kept_ref, place_ref,
               rows_ref, twiddle_ref, common_ref, first_ref, second_ref, owner_ref, parts_ref, sems):
    sources = (rows_any, twiddle_any, common_any, first_any, second_any, owner_any)
    targets = (rows_ref, twiddle_ref, common_ref, first_ref, second_ref, owner_ref)
    copies = [pltpu.make_async_copy(s, t, sems.at[i]) for i, (s, t) in enumerate(zip(sources, targets))]
    for copy in copies:
        copy.start()
    for copy in copies:
        copy.wait()

    owner = owner_ref[...]
    lanes = jnp.broadcast_to(owner, (PAIRS, PAIRS)).astype(jnp.float32)
    earlier = lax.broadcasted_iota(jnp.int32, (PAIRS, PAIRS), 0) < lax.broadcasted_iota(jnp.int32, (PAIRS, PAIRS), 1)
    same = (lanes == lanes.T) & earlier
    slot = jnp.sum(same.astype(jnp.float32), axis=0, keepdims=True).astype(jnp.int32)
    place_ref[...] = one_hot([owner * CAP + slot], place_ref.shape[0]).astype(jnp.bfloat16)
    second = second_ref[...]
    second = second + (second >> 3) * (SLAB - SENSORS)
    kept_ref[RES] = jnp.zeros(kept_ref.shape[1:], jnp.bfloat16)
    kept_ref[RES, pl.ds(0, PICKED), pl.ds(0, TILE)] = one_hot([second + c * SENSORS for c in range(COMPS)], TILE).T.astype(jnp.bfloat16)
    pick_first = one_hot([first_ref[...] + c * SENSORS for c in range(COMPS)], TILE).T.astype(jnp.bfloat16)[:, :SLAB]

    def store(k, value):
        value = padded(value)
        kept_ref[k, pl.ds(PICKED, SLAB), :] = value
        first = jnp.dot(pick_first, value, preferred_element_type=jnp.float32)
        kept_ref[k, pl.ds(0, PICKED), :] = first.astype(jnp.bfloat16)

    forward(lambda columns: rows_ref[:, columns], twiddle_ref, common_ref, parts_ref, store)


def farther_kernel(rows_ref, twiddle_ref, common_ref, white_ref, parts_ref):
    def store(k, value):
        white_ref[k] = padded(value)

    forward(lambda columns: rows_ref[:, columns], twiddle_ref, common_ref, parts_ref, store)


def nearer_kernel(sibling_ref, passed_ref, twiddle_ref, common_ref, white_ref, parts_ref):
    odd = lax.axis_index("sens") & 1

    def store(k, value):
        white_ref[k] = padded(value)

    for parity, rows_ref in ((0, sibling_ref), (1, passed_ref)):
        @pl.when(odd == parity)
        def _(rows_ref=rows_ref):
            forward(lambda columns: rows_ref[:, columns], twiddle_ref, common_ref, parts_ref, store)


def shares(distances, hour, kept_ref, second_rows_ref, cosines_ref, sines_ref, flip_ref, out_refs, cross_ref, tile_ref,
           prepare=lambda k: None):
    count = cross_ref.shape[0]
    base = ((hour ^ distances[0]) >> 2) * (count - 1)
    comps = [base + i for i in range(count)]
    firsts = [lax.div(i, COMPS) for i in comps]
    seconds = [i - f * COMPS for i, f in zip(comps, firsts)]
    group = 16

    def cross(k):
        for g in range(0, PAIRS, group):
            def load(ref, index):
                at = pl.ds(pl.multiple_of(index * PAIRS + g, group), group)
                return ref[k, at, :].astype(jnp.float32)

            first_of = {i: load(kept_ref, firsts[i]) for i in (0, 2, 4)}
            second_of = {i: load(second_rows_ref, seconds[i]) for i in (0, 1, 2)}
            at = pl.ds(g, group)
            for i, (f, s) in enumerate(((0, 0), (0, 1), (2, 2), (4, 0), (4, 1))):
                ar, ai = first_of[f][:, :BINS], first_of[f][:, BINS:]
                br, bi = second_of[s][:, :BINS], second_of[s][:, BINS:]
                cross_ref[i, at, pl.ds(k * BINS, BINS)] = (ar * br + ai * bi).astype(jnp.bfloat16)
                cross_ref[i, at, pl.ds(NB + k * BINS, BINS)] = (ar * bi - ai * br).astype(jnp.bfloat16)

    def rows(start, width):
        return cross_ref[:, :, pl.ds(start, width)].reshape(count * PAIRS, width)

    def plus(x, y):
        return y if x is None else x + y

    steps = 4
    each = RES // steps
    width = NB // steps
    even = odd = zero = None
    for step in range(steps + 1):
        for k in range(each * 2) if step == 0 else range((step + 1) * each, min((step + 2) * each, RES)):
            prepare(k)
        for k in range(step * each, min((step + 1) * each, RES)):
            cross(k)
        if step:
            at = (step - 1) * width
            real_part, imag_part = rows(at, width), rows(NB + at, width)
            even = plus(even, jnp.dot(real_part, cosines_ref[pl.ds(at, width), :], preferred_element_type=jnp.float32))
            odd = plus(odd, jnp.dot(imag_part, sines_ref[pl.ds(at, width), :], preferred_element_type=jnp.float32))
            zero = plus(zero, jnp.sum(real_part.astype(jnp.float32), axis=1, keepdims=True))
    later = pltpu.roll(even - odd, 1, axis=1)
    start = lax.broadcasted_iota(jnp.int32, later.shape, 1) == 0
    after = jnp.where(start, zero, later).astype(jnp.bfloat16)
    before = (even + odd).astype(jnp.bfloat16)
    per_comp, per_half = LAGS // TILE, HALF // TILE
    for tile in range(per_half):
        at = tile * TILE
        turned = jnp.dot(before[:, at : at + TILE], flip_ref[...], preferred_element_type=jnp.float32)
        turned = turned.astype(jnp.bfloat16)
        for c in range(count):
            of = slice(c * PAIRS, (c + 1) * PAIRS)
            tile_ref[c * per_comp + per_half - 1 - tile] = turned[of]
            tile_ref[c * per_comp + per_half + tile] = after[of, at : at + TILE]
    for distance, out_ref in zip(distances, out_refs):
        tiles = out_ref.shape[1] // TILE
        begin = (hour ^ distance) * tiles - base * per_comp
        for u in range(tiles):
            out_ref[:, u * TILE : (u + 1) * TILE] = tile_ref[begin + u]


def across_kernel(distances, kept_ref, near_ref, far_ref, cosines_ref, sines_ref, flip_ref, *refs):
    *out_refs, second_rows_ref, cross_ref, tile_ref = refs
    pick = kept_ref[RES, pl.ds(0, PICKED), pl.ds(0, TILE)][:, : 3 * SLAB]

    def prepare(k):
        spectra = jnp.concatenate([kept_ref[k, pl.ds(PICKED, SLAB), :], near_ref[k], far_ref[k]], axis=0)
        second = jnp.dot(pick, spectra, preferred_element_type=jnp.float32)
        second_rows_ref[k] = second.astype(jnp.bfloat16)

    shares(distances, lax.axis_index("hour"), kept_ref, second_rows_ref, cosines_ref, sines_ref, flip_ref, out_refs, cross_ref,
           tile_ref, prepare)


def along_kernel(distances, kept_ref, second_rows_ref, cosines_ref, sines_ref, flip_ref, *refs):
    *out_refs, cross_ref, tile_ref = refs
    shares(distances, lax.axis_index("hour"), kept_ref, second_rows_ref, cosines_ref, sines_ref, flip_ref, out_refs, cross_ref,
           tile_ref)


def total_of(parts_refs):
    total = parts_refs[0][...].astype(jnp.float32)
    for ref in parts_refs[1:]:
        total = total + ref[...].astype(jnp.float32)
    return total


def fold_kernel(*refs):
    *parts_refs, out_ref = refs
    out_ref[...] = total_of(parts_refs).astype(jnp.bfloat16)


def collect_kernel(place_ref, *refs):
    *parts_refs, out_ref = refs
    total = (total_of(parts_refs) * (1.0 / 128.0)).astype(jnp.bfloat16)
    out_ref[...] = jnp.dot(place_ref[...], total, preferred_element_type=jnp.float32).astype(jnp.bfloat16)


def shards(windows, pair_first, pair_second, owners):
    twiddle, common, cosines, sines, flip = (jnp.asarray(t) for t in tables())
    hours = lax.axis_size("hour")
    share = COMPS * COMPS * LAGS // hours
    slots = lax.axis_size("sens") * CAP
    bf16, f32, i32 = jnp.bfloat16, jnp.float32, jnp.int32
    rows = windows[0].transpose(1, 0, 2).reshape(ROWS, SAMPLES)
    sens = lax.axis_size("sens")
    swap = [(s, s ^ 1) for s in range(sens)]
    farther = lax.ppermute(rows, "sens", [(s, (s - 2) % sens) for s in range(sens)])
    sibling = lax.ppermute(rows, "sens", swap)

    vmem = pl.BlockSpec(memory_space=pltpu.VMEM)
    hbm = pl.BlockSpec(memory_space=pltpu.HBM)
    parts_scratch = pltpu.VMEM((RES * ROWS, 2 * SPAN), f32)
    params = pltpu.CompilerParams(vmem_limit_bytes=16 * MIB)

    spectra = jax.ShapeDtypeStruct((RES, SLAB, 2 * BINS), bf16)

    def cost(flops):
        return pl.CostEstimate(flops=flops, bytes_accessed=10**6, transcendentals=0)

    kept, place = pl.pallas_call(
        own_kernel,
        out_shape=(
            pltpu.VMEM((RES + 1, PICKED + SLAB, 2 * BINS), bf16),
            pltpu.VMEM((slots, PAIRS), bf16),
        ),
        in_specs=[hbm] * 6,
        out_specs=(vmem,) * 2,
        scratch_shapes=[
            pltpu.VMEM((ROWS, SAMPLES), bf16),
            pltpu.VMEM(twiddle.shape, f32),
            pltpu.VMEM(common.shape, bf16),
            pltpu.VMEM((1, PAIRS), i32),
            pltpu.VMEM((1, PAIRS), i32),
            pltpu.VMEM((1, PAIRS), i32),
            parts_scratch,
            pltpu.SemaphoreType.DMA((6,)),
        ],
        compiler_params=pltpu.CompilerParams(vmem_limit_bytes=56 * MIB),
        cost_estimate=cost(10000000000),
        name="own",
    )(rows, twiddle, common, *(v.reshape(1, PAIRS) for v in (pair_first, pair_second, owners)))
    farther, place = lax.optimization_barrier((farther, place))
    passed = lax.ppermute(farther, "sens", swap)

    def whitened(kernel, name, in_specs, args):
        return pl.pallas_call(
            kernel,
            out_shape=spectra,
            in_specs=in_specs,
            out_specs=vmem,
            scratch_shapes=[parts_scratch],
            compiler_params=params,
            cost_estimate=cost(700000000),
            name=name,
        )(*args, twiddle, common)

    far = whitened(farther_kernel, "farther", [vmem] * 3, (farther,))
    near = whitened(nearer_kernel, "nearer", [vmem] * 4, (sibling, passed))
    one = jax.ShapeDtypeStruct((PAIRS, share), bf16)
    half = COMPS * COMPS // 2 + 1
    shares_scratch = [pltpu.VMEM((half, PAIRS, 2 * NB), bf16), pltpu.VMEM((half * LAGS // TILE, PAIRS, TILE), bf16)]
    big = pltpu.CompilerParams(vmem_limit_bytes=24 * MIB)
    other, same = (7, 6, 5, 4), (3, 2, 1, 0)
    *across, second_rows = pl.pallas_call(
        functools.partial(across_kernel, other),
        out_shape=(one,) * 4 + (jax.ShapeDtypeStruct((RES, PICKED, 2 * BINS), bf16),),
        in_specs=[vmem] * 6,
        out_specs=(vmem,) * 5,
        scratch_shapes=shares_scratch,
        compiler_params=big,
        cost_estimate=cost(3 * 10**9),
        name="across",
    )(kept, near, far, cosines, sines, flip)
    along = pl.pallas_call(
        functools.partial(along_kernel, same),
        out_shape=(one,) * 4,
        in_specs=[vmem] * 5,
        out_specs=(vmem,) * 4,
        scratch_shapes=shares_scratch,
        compiler_params=big,
        cost_estimate=cost(3 * 10**9),
        name="along",
    )(kept, second_rows, cosines, sines, flip)
    def exchanged(part, distance):
        return lax.ppermute(part, "hour", [(h, h ^ distance) for h in range(hours)]) if distance else part

    def fold(*shares_here):
        return pl.pallas_call(
            fold_kernel,
            out_shape=one,
            in_specs=[vmem] * len(shares_here),
            out_specs=vmem,
            compiler_params=params,
            cost_estimate=cost(10**7),
            name="fold",
        )(*shares_here)

    far_y, far_two, far_one, far_here = across
    same_y, same_two, same_one, same_here = along
    joined = exchanged(far_two, 4)
    folded = fold(exchanged(far_y, 3), exchanged(far_one, 1), far_here)
    parts = [
        exchanged(folded, 4),
        exchanged(same_y, 3),
        exchanged(same_one, 1),
        exchanged(fold(same_two, joined), 2),
        same_here,
    ]
    outgoing = pl.pallas_call(
        collect_kernel,
        out_shape=jax.ShapeDtypeStruct((slots, share), bf16),
        in_specs=[vmem] * (1 + len(parts)),
        out_specs=vmem,
        compiler_params=params,
        cost_estimate=cost(2 * 10**7),
        name="collect",
    )(place, *parts)
    stacked = lax.all_to_all(outgoing, "sens", split_axis=0, concat_axis=0, tiled=True)
    return stacked.astype(jnp.float32)


def solution(mesh):
    placed = (P("hour", "sens", None, None), P("sens"), P("sens"), P("sens", None))
    return jax.shard_map(
        shards, mesh=mesh, in_specs=placed, out_specs=P("sens", "hour"), check_vma=False
    )
```
